32 devices in a mesh: hidden: 4 (over z), width: 2 (over x), replica: 4 (over y, core).
Axes of the slice: x: 2, y: 2, z: 4, core: 2. Of those that a mesh axis runs over, the one named last changes fastest.
Arguments:
- saved_input: bfloat16 [1024, 12288], P(('replica', 'hidden'), 'width'), may hold values from -0.19921875 to 0.19921875
- grad_out: bfloat16 [1024, 24576], P(('replica', 'width'), 'hidden'), may hold values from -6 to 6
- weight: bfloat16 [12288, 24576], P('width', 'hidden'), may hold values from -0.0546875 to 0.0546875
- samples: int32 [64], replicated, may hold values from 8 to 16
- correct: int32 [64], replicated, may hold values from 0 to 8
- prompt_ids: int32 [1024], P('replica'), may hold values from 0 to 63
Outputs:
- grad_input: bfloat16 [1024, 12288], P(('replica', 'hidden'), 'width')
- grad_weight: float32 [12288, 24576], P(('width', 'replica'), 'hidden')
The draws below stay inside these ranges and needn't reach their ends.
Inputs may be any that keep to these rules, and one draw needn't show every extreme that they name: correct[i] <= samples[i] for every prompt.
All inputs are finite; a program needn't handle non-finite values.
Results may differ from the reference program's by a relative error of at most 0.012.
Values may be sent and summed in bfloat16 or wider, within the bound.
No kernel may reach another device: no remote copies, remote signals or barrier semaphores. Data moves between devices by JAX's collectives and lax.ppermute only.
A program may use at most 320 MiB of HBM per device.

```python
import jax
import jax.numpy as jnp
from jax import lax

D = 12288
FF = 24576
TOK_REP = 256
PROMPTS = 64
K = 4
TOKENS = 1024
N_REPLICA = 4


def place_ends(entries, own_key, low, high):
    index_at = [jax.random.randint(jax.random.fold_in(own_key, axis), (), 0, length) for axis, length in enumerate(entries.shape)]
    main_axis = entries.shape.index(max(entries.shape))
    beside = index_at[:main_axis] + [(index_at[main_axis] + 1) % entries.shape[main_axis]] + index_at[main_axis + 1:]
    return entries.at[tuple(index_at)].set(low).at[tuple(beside)].set(high)


def with_spikes(result, own_key, source, target, blocks, factor):
    def block_of(dim):
        return (jnp.arange(result.shape[dim]) // (result.shape[dim] // blocks)).reshape((-1,) + (1,) * (result.ndim - 1 - dim))

    one_side = jax.random.permutation(own_key, blocks)[block_of(target)]
    second = (block_of(target) + blocks // 2) % blocks
    return jnp.where((block_of(source) == one_side) | (block_of(source) == second), factor * result, result)


def block_levels(stream_key, shape, split, least, largest):
    level, own = 1.0, jax.random.fold_in(stream_key, 6)
    for position, parts in split:
        steps = jnp.exp(jax.random.uniform(jax.random.fold_in(own, position), (parts,), jnp.float32, least / len(split), largest / len(split)))
        level = level * jnp.repeat(steps, shape[position] // parts).reshape([-1 if axis == position else 1 for axis in range(len(shape))])
    return level


def noise(key, extent, scale, most, shards=(), kind=jnp.bfloat16):
    gain = block_levels(key, extent, shards, -0.22, 0.18) if shards else 1.0
    drawn = jax.random.normal(key, extent, jnp.float32) * scale * gain
    return jnp.minimum(jnp.maximum(drawn, -most), most).astype(kind)


def bell_draw_with(stream_key, dims, deviation, reach, split, heavy, dtype=jnp.bfloat16):
    values = deviation * jax.random.normal(stream_key, dims, jnp.float32)
    if split:
        values = values * block_levels(stream_key, dims, split, -0.22, 0.18)
    return jnp.clip(with_spikes(values, jax.random.fold_in(stream_key, 3), *heavy), -reach, reach).astype(dtype)


def setup_inputs(seed: int = 0) -> dict:
    seeds = jax.random.split(jax.random.key(seed), 7)
    return {
        "saved_input": bell_draw_with(seeds[0], (TOKENS, D), 0.03, 0.19921875, ((0, 16), (1, 2)), (0, 1, 16, 2.0)),
        "grad_out": bell_draw_with(seeds[1], (TOKENS, FF), 1.0, 6.0, ((0, 8), (1, 4)), (1, 0, 8, 2.0)),
        "weight": noise(seeds[2], (D, FF), D ** -0.5, 0.0546875, ((0, 2), (1, 4))),
        "samples": place_ends(jax.random.randint(seeds[3], (PROMPTS,), 8, 17), jax.random.fold_in(seeds[3], 1), 8, 16).astype(jnp.int32),
        "correct": place_ends(jax.random.randint(seeds[4], (PROMPTS,), 0, 9), jax.random.fold_in(seeds[4], 1), 0, 8).astype(jnp.int32),
        "prompt_ids": place_ends(jax.random.randint(seeds[5], (TOKENS,), 0, PROMPTS), jax.random.fold_in(seeds[5], 1), 0, PROMPTS - 1).astype(jnp.int32),
    }


def pass_weights(samples, correct):
    total = samples.astype(jnp.float32)
    good = correct.astype(jnp.float32)
    missing = jnp.ones_like(total)
    for factor_index in range(K):
        missing = missing * jnp.maximum(total - good - factor_index, 0.0) / (total - factor_index)
    return 1.0 - missing


def reference(saved_input, grad_out, weight, samples, correct, prompt_ids):
    pass_at_k = pass_weights(samples, correct)
    token_weight = lax.optimization_barrier(pass_at_k[prompt_ids].astype(jnp.bfloat16))
    scaled = (grad_out.astype(jnp.float32) * token_weight.astype(jnp.float32)[:, None]).astype(jnp.bfloat16)
    grad_input = lax.dot_general(scaled, weight, (((1,), (1,)), ((), ())), preferred_element_type=jnp.float32).astype(jnp.bfloat16)
    input_groups = saved_input.reshape(N_REPLICA, TOK_REP, D)
    scaled_groups = scaled.reshape(N_REPLICA, TOK_REP, FF)

    def accumulate(total, pair):
        partial_sum = lax.dot_general(pair[0], pair[1], (((0,), (0,)), ((), ())), preferred_element_type=jnp.float32)
        rounded = lax.optimization_barrier(partial_sum.astype(jnp.bfloat16))
        return total + rounded.astype(jnp.float32), None

    grad_weight, _ = lax.scan(accumulate, jnp.zeros((D, FF), jnp.float32), (input_groups, scaled_groups))
    return grad_input, grad_weight
```

```python
import functools

import jax
import jax.numpy as jnp
from jax import lax
from jax.experimental import pallas as pl
from jax.experimental.pallas import tpu as pltpu
from jax.sharding import PartitionSpec as P

K = 4


def pass_weights(samples, correct):
    total = samples.astype(jnp.float32)
    good = correct.astype(jnp.float32)
    missing = jnp.ones_like(total)
    for factor_index in range(K):
        missing = missing * jnp.maximum(total - good - factor_index, 0.0) / (total - factor_index)
    return 1.0 - missing


def token_weights(prompt_ids, samples, correct):
    pass_at_k = pass_weights(samples, correct)
    prompt_range = jnp.arange(samples.shape[0], dtype=jnp.int32)
    matches = prompt_ids[:, None] == prompt_range[None, :]
    picked = jnp.sum(jnp.where(matches, pass_at_k[None, :], 0.0), axis=1, keepdims=True)
    rounded = lax.optimization_barrier(picked.astype(jnp.bfloat16))
    return rounded.astype(jnp.float32)


def after(value, *others):
    return lax.optimization_barrier((value,) + others)[0]


def weight_grad_kernel(place_ref, *refs, n_x, n_s, n_h):
    x_refs, s_refs, out_ref, x_all, s_all = refs[:n_x], refs[n_x:n_x + n_s], refs[-3], refs[-2], refs[-1]
    rows = s_refs[0].shape[0]
    groups = x_refs[0].shape[0] // rows

    @pl.when(pl.program_id(0) == 0)
    def _():
        for k in range(n_x):
            @pl.when(place_ref[k] >= 0)
            def _(k=k):
                for g in range(groups):
                    start = pl.multiple_of((g * n_h + place_ref[k]) * rows, rows)
                    x_all[pl.ds(start, rows), :] = x_refs[k][g * rows:(g + 1) * rows, :]

    for k in range(n_s):
        s_all[k * rows:(k + 1) * rows, :] = s_refs[k][...]
    out_ref[...] = lax.dot_general(
        x_all[...], s_all[...], (((0,), (0,)), ((), ())), preferred_element_type=jnp.float32
    )


def weight_grad(places, x_pieces, s_pieces, n_h):
    x_rows, m = x_pieces[0].shape
    rows, f = s_pieces[0].shape
    tokens = rows * len(s_pieces)
    block = 512 if f % 512 == 0 else f
    body = functools.partial(weight_grad_kernel, n_x=len(x_pieces), n_s=len(s_pieces), n_h=n_h)
    return pl.pallas_call(
        body,
        grid_spec=pltpu.PrefetchScalarGridSpec(
            num_scalar_prefetch=1,
            grid=(f // block,),
            in_specs=[pl.BlockSpec((x_rows, m), lambda j, p: (0, 0))] * len(x_pieces)
            + [pl.BlockSpec((rows, block), lambda j, p: (0, j))] * len(s_pieces),
            out_specs=pl.BlockSpec((m, block), lambda j, p: (0, j)),
            scratch_shapes=[pltpu.VMEM((tokens, m), jnp.bfloat16), pltpu.VMEM((tokens, block), jnp.bfloat16)],
        ),
        out_shape=jax.ShapeDtypeStruct((m, f), jnp.float32),
        compiler_params=pltpu.CompilerParams(vmem_limit_bytes=56 << 20),
        cost_estimate=pl.CostEstimate(
            flops=2 * m * f * tokens, bytes_accessed=2 * tokens * (m + f) + 4 * m * f, transcendentals=0
        ),
    )(places, *x_pieces, *s_pieces)


def make_body(n_h, n_w, n_r):
    n_c = 2 if n_r % 2 == 0 else 1
    n_y = n_r // n_c
    per_w = n_h // n_w

    def slot(w_index, group):
        return group if w_index < n_w // 2 else per_w - 1 - group

    def slot_of(w_index, group):
        return jnp.where(w_index < n_w // 2, group, per_w - 1 - group)

    def replica_perm(dy, dc):
        return [
            (y * n_c + c, (y + dy) % n_y * n_c + (c + dc) % n_c) for y in range(n_y) for c in range(n_c)
        ]

    def over_replica(value, dy, dc):
        return lax.ppermute(value, "replica", replica_perm(dy, dc))

    def over_width(value, dx):
        return lax.ppermute(value, "width", [(w, (w + dx) % n_w) for w in range(n_w)])

    def body(saved_input, grad_out, weight, samples, correct, prompt_ids):
        h, w, r = lax.axis_index("hidden"), lax.axis_index("width"), lax.axis_index("replica")
        y, c = r // n_c, r % n_c
        x_rows, d_half = saved_input.shape
        s_rows, f = grad_out.shape
        rows = s_rows // per_w
        d_core = d_half // n_c
        d_own = d_half // n_r

        parts = []
        for dy in range(n_y):
            for dc in range(n_c):
                target = (y + dy) % n_y * n_c + (c + dc) % n_c
                part = lax.dynamic_slice_in_dim(saved_input, target * d_own, d_own, 1)
                parts.append(part if dy == dc == 0 else over_replica(part, dy, dc))
        x_own = jnp.concatenate(parts, axis=0)

        all_weights = token_weights(prompt_ids, samples, correct)
        s = {}
        for q in range(per_w):
            start = slot_of(w, q) * rows
            g = lax.dynamic_slice_in_dim(grad_out, start, rows, 0).astype(jnp.float32)
            scale = lax.dynamic_slice_in_dim(all_weights, w * s_rows + start, rows, 0)
            s[0, 0, 0, q] = (g * scale).astype(jnp.bfloat16)

        def spread_cores(dy, dx, q):
            for dc in range(1, n_c):
                s[dy, dc, dx, q] = over_replica(s[dy, 0, dx, q], 0, dc)

        for q in range(per_w):
            spread_cores(0, 0, q)
        last = ()
        for q in range(per_w):
            own = after(s[0, 0, 0, q], *last) if last else s[0, 0, 0, q]
            last = ()
            for dx in range(1, n_w):
                s[0, 0, dx, q] = over_width(own, dx)
                last += (s[0, 0, dx, q],)
            for dy in range(1, n_y):
                s[dy, 0, 0, q] = over_replica(own, dy, 0)
            for dx in range(1, n_w):
                spread_cores(0, dx, q)
            for dy in range(1, n_y):
                spread_cores(dy, 0, q)
        for dy in range(1, n_y):
            for dx in range(1, n_w):
                for q in range(per_w):
                    if q % 2 == 0:
                        s[dy, 0, dx, q] = over_width(after(s[dy, 0, 0, q], *last), dx)
                    else:
                        s[dy, 0, dx, q] = over_replica(s[0, 0, dx, q], dy, 0)
                    spread_cores(dy, dx, q)

        right, left = [x_own], [x_own]
        for k in range(1, n_h):
            right.append(lax.ppermute(right[-1], "hidden", [(j, j + 1) for j in range(k - 1, n_h - 1)]))
            left.append(lax.ppermute(left[-1], "hidden", [(j, j - 1) for j in range(1, n_h - k + 1)]))

        own_weight = lax.dynamic_slice_in_dim(weight, c * d_core, d_core, 0)
        shares = []
        for q in range(per_w):
            tokens = jnp.concatenate([s[0, dc, dx, q] for dc in range(n_c) for dx in range(n_w)], axis=0)
            share = lax.dot_general(
                tokens, own_weight, (((1,), (1,)), ((), ())), preferred_element_type=jnp.float32
            )
            shares.append(share.reshape(n_c, n_w, rows, d_core))

        def share_of(target, choices):
            target = jnp.clip(target, 0, n_h - 1)
            owner, group = target // per_w, target % per_w
            dx, q = (w - owner) % n_w, slot_of(owner, group)
            picked = None
            for choice in choices:
                value = lax.dynamic_index_in_dim(shares[choice], dx, 1, keepdims=False)
                picked = value if picked is None else jnp.where(q == choice, value, picked)
            return picked

        def passes(targets):
            return sorted({slot(t // per_w, t % per_w) for t in targets})

        from_left = from_right = None
        for step in range(1, n_h):
            apart = n_h - step
            choices = passes([j + apart for j in range(step)] + [j - apart for j in range(apart, n_h)])
            to_right, to_left = share_of(h + apart, choices), share_of(h - apart, choices)
            if step > 1:
                to_right = to_right + from_left.astype(jnp.float32)
                to_left = to_left + from_right.astype(jnp.float32)
            from_left = lax.ppermute(
                to_right.astype(jnp.bfloat16), "hidden", [(j, j + 1) for j in range(step)]
            )
            from_right = lax.ppermute(
                to_left.astype(jnp.bfloat16), "hidden", [(j, j - 1) for j in range(apart, n_h)]
            )
        total = share_of(h, range(per_w)) + from_left.astype(jnp.float32) + from_right.astype(jnp.float32)
        total = total.astype(jnp.bfloat16)
        held = [total[0]] + [over_replica(total[dc], 0, n_c - dc) for dc in range(1, n_c)]
        held = jnp.stack(held)
        grad_input = jnp.concatenate(
            [lax.dynamic_index_in_dim(held, (p - c) % n_c, 0, keepdims=False) for p in range(n_c)], axis=1
        )

        places, pieces = [], []
        for k in range(n_h):
            for plane, piece, there in (
                (h - k, right[k], h >= k),
                (h + k, left[k], (h + k < n_h) & (k > 0)),
            ):
                if k == 0 and piece is left[0] and len(pieces) == 1:
                    continue
                owner, group = plane // per_w, plane % per_w
                place = (w - owner) % n_w * per_w + slot_of(owner, group)
                places.append(jnp.where(there, place, -1).astype(jnp.int32))
                pieces.append(piece)
        s_pieces = [
            s[dy, dc, dx, q] for dy in range(n_y) for dc in range(n_c) for dx in range(n_w) for q in range(per_w)
        ]
        grad_weight = weight_grad(jnp.stack(places), pieces, s_pieces, n_h)
        return grad_input, grad_weight

    return body


def solution(mesh):
    in_specs = (
        P(("replica", "hidden"), "width"),
        P(("replica", "width"), "hidden"),
        P("width", "hidden"),
        P(),
        P(),
        P("replica"),
    )
    out_specs = (P(("replica", "hidden"), "width"), P(("width", "replica"), "hidden"))
    body = make_body(mesh.shape["hidden"], mesh.shape["width"], mesh.shape["replica"])
    return jax.shard_map(body, mesh=mesh, in_specs=in_specs, out_specs=out_specs, check_vma=False)
```

```python
import functools

import jax
import jax.numpy as jnp
from jax import lax
from jax.experimental import pallas as pl
from jax.experimental.pallas import tpu as pltpu
from jax.sharding import PartitionSpec as P

K = 4
CDW = 2
CDX = 0
VMEM = 60 << 20


def pass_weights(samples, correct):
    total = samples.astype(jnp.float32)
    good = correct.astype(jnp.float32)
    missing = jnp.ones_like(total)
    for factor_index in range(K):
        missing = missing * jnp.maximum(total - good - factor_index, 0.0) / (total - factor_index)
    return 1.0 - missing


def token_weights(prompt_ids, samples, correct):
    pass_at_k = pass_weights(samples, correct)
    prompt_range = jnp.arange(samples.shape[0], dtype=jnp.int32)
    matches = prompt_ids[:, None] == prompt_range[None, :]
    picked = jnp.sum(jnp.where(matches, pass_at_k[None, :], 0.0), axis=1, keepdims=True)
    rounded = lax.optimization_barrier(picked.astype(jnp.bfloat16))
    return rounded.astype(jnp.float32)


def COST_DW(m, f, tokens):
    return pl.CostEstimate(flops=CDW * m * f * tokens, bytes_accessed=CDW * (tokens * (m + f) + 2 * m * f), transcendentals=0)


def COST_DX(n, f, width):
    return pl.CostEstimate(flops=CDX * n * f * width, bytes_accessed=CDX * f * (width + n), transcendentals=0)


def after(value, *others):
    return lax.optimization_barrier((value,) + others)[0]


def weight_grad_kernel(place_ref, *refs, n_x, n_s, n_h, rows):
    x_refs, s_refs, out_ref, x_all, s_all = refs[:n_x], refs[n_x:n_x + n_s], refs[-3], refs[-2], refs[-1]
    groups = x_refs[0].shape[0] // rows

    @pl.when(pl.program_id(0) == 0)
    def _():
        for k in range(n_x):
            @pl.when(place_ref[k * groups] >= 0)
            def _(k=k):
                for g in range(groups):
                    start = pl.multiple_of((g * n_h + place_ref[k * groups + g]) * rows, rows)
                    x_all[pl.ds(start, rows), :] = x_refs[k][g * rows:(g + 1) * rows, :]

    start = 0
    for s_ref in s_refs:
        s_all[start:start + s_ref.shape[0], :] = s_ref[...]
        start += s_ref.shape[0]
    out_ref[...] = lax.dot_general(
        x_all[...], s_all[...], (((0,), (0,)), ((), ())), preferred_element_type=jnp.float32
    )


def column_block(f):
    return next((b for b in (1024, 512, 256, 128) if f % b == 0 and f // b > 2), f)


def weight_grad(places, x_pieces, s_pieces, n_h, rows, due):
    x_rows, m = x_pieces[0].shape
    f = s_pieces[0].shape[1]
    tokens = x_rows * n_h
    block = column_block(f)
    body = functools.partial(weight_grad_kernel, n_x=len(x_pieces), n_s=len(s_pieces), n_h=n_h, rows=rows)
    return pl.pallas_call(
        body,
        grid_spec=pltpu.PrefetchScalarGridSpec(
            num_scalar_prefetch=1,
            grid=(f // block,),
            in_specs=[pl.BlockSpec((x_rows, m), lambda j, p: (0, 0))] * len(x_pieces)
            + [pl.BlockSpec((piece.shape[0], block), lambda j, p: (0, j)) for piece in s_pieces],
            out_specs=pl.BlockSpec((m, block), lambda j, p: (0, j)),
            scratch_shapes=[pltpu.VMEM((tokens, m), jnp.bfloat16), pltpu.VMEM((tokens, block), jnp.bfloat16)],
        ),
        out_shape=jax.ShapeDtypeStruct((m, f), jnp.float32),
        compiler_params=pltpu.CompilerParams(vmem_limit_bytes=VMEM),
        cost_estimate=COST_DW(m, f, tokens),
    )(after(places, *due) if due else places, *x_pieces, *s_pieces)


def input_grad_kernel(first_ref, *refs):
    piece_refs, weight_ref, out_ref, tokens = refs[:-3], refs[-3], refs[-2], refs[-1]
    rows = piece_refs[0].shape[0]

    @pl.when(pl.program_id(0) == 0)
    def _():
        for k, piece_ref in enumerate(piece_refs):
            tokens[k * rows:(k + 1) * rows, :] = piece_ref[...]

    share = lax.dot_general(
        tokens[...], weight_ref[...], (((1,), (1,)), ((), ())), preferred_element_type=jnp.float32
    ).astype(out_ref.dtype)
    per_owner = out_ref.shape[2]
    for k in range(out_ref.shape[0]):
        out_ref[k, 0] = share[k * per_owner:(k + 1) * per_owner]


def input_grad(core, n_c, rows, pieces, weight, owners, parts, due):
    d, f = weight.shape
    width = d // n_c
    n = rows * len(pieces)
    part = width // parts
    block = next(b for b in (512, 256, 128, part) if part % b == 0)
    per_part = part // block
    steps = width // block
    first = jnp.stack([core * steps] + [index for _, index in pieces]).astype(jnp.int32)
    return pl.pallas_call(
        input_grad_kernel,
        grid_spec=pltpu.PrefetchScalarGridSpec(
            num_scalar_prefetch=1,
            grid=(steps,),
            in_specs=[pl.BlockSpec((rows, f), lambda j, c, k=k: (c[k + 1], 0)) for k in range(len(pieces))]
            + [pl.BlockSpec((block, f), lambda j, c: (c[0] + j, 0))],
            out_specs=pl.BlockSpec(
                (owners, 1, n // owners, block), lambda j, c: (0, j // per_part, 0, j % per_part)
            ),
            scratch_shapes=[pltpu.VMEM((n, f), jnp.bfloat16)],
        ),
        out_shape=jax.ShapeDtypeStruct((owners, parts, n // owners, part), jnp.bfloat16),
        compiler_params=pltpu.CompilerParams(vmem_limit_bytes=VMEM),
        cost_estimate=COST_DX(n, f, width),
    )(after(first, *due) if due else first, *[piece for piece, _ in pieces], weight)


def make_body(n_h, n_w, n_r):
    n_c = 2 if n_r % 2 == 0 else 1
    n_y = n_r // n_c
    per_w = n_h // n_w

    def slot(w_index, group):
        return group if w_index < n_w // 2 else per_w - 1 - group

    def slot_of(w_index, group):
        return jnp.where(w_index < n_w // 2, group, per_w - 1 - group)

    def replica_perm(dy, dc):
        return [
            (y * n_c + c, (y + dy) % n_y * n_c + (c + dc) % n_c) for y in range(n_y) for c in range(n_c)
        ]

    def over_replica(value, dy, dc):
        return lax.ppermute(value, "replica", replica_perm(dy, dc))

    def over_width(value, dx):
        return lax.ppermute(value, "width", [(w, (w + dx) % n_w) for w in range(n_w)])

    def body(saved_input, grad_out, weight, samples, correct, prompt_ids):
        h, w, r = lax.axis_index("hidden"), lax.axis_index("width"), lax.axis_index("replica")
        y, c = r // n_c, r % n_c
        x_rows, d_half = saved_input.shape
        s_rows, f = grad_out.shape
        rows = s_rows // per_w
        d_core = d_half // n_c
        d_own = d_half // n_r

        parts = []
        for dy in range(n_y):
            for dc in range(n_c):
                target = (y + dy) % n_y * n_c + (c + dc) % n_c
                part = lax.dynamic_slice_in_dim(saved_input, target * d_own, d_own, 1)
                parts.append(part if dy == dc == 0 else over_replica(part, dy, dc))
        x_own = jnp.concatenate(parts, axis=0)

        all_weights = token_weights(prompt_ids, samples, correct)
        scale = lax.dynamic_slice_in_dim(all_weights, w * s_rows, s_rows, 0)
        scaled = (grad_out.astype(jnp.float32) * scale).astype(jnp.bfloat16)

        own_group = [lax.dynamic_slice_in_dim(scaled, slot_of(w, q) * rows, rows, 0) for q in range(per_w)]

        def spread(value, *late):
            value = after(value, *late) if late else value
            return [value] + [over_replica(value, 0, dc) for dc in range(1, n_c)]

        whole = spread(scaled, *parts[1:n_c])
        x_own = after(x_own, *whole[1:])
        piece, cores = {}, {}

        def send_x(q, *late):
            own = after(own_group[q], *late) if late else own_group[q]
            for dx in range(1, n_w):
                piece[0, dx, q] = over_width(own, dx)

        def send_y(q, *late):
            own = after(own_group[q], *late)
            for dy in range(1, n_y):
                piece[dy, 0, q] = over_replica(own, dy, 0)

        def send_on(q, *late):
            for dy in range(1, n_y):
                for dx in range(1, n_w):
                    if q % 2 == 0:
                        piece[dy, dx, q] = over_width(after(piece[dy, 0, q], *late), dx)
                    else:
                        piece[dy, dx, q] = over_replica(after(piece[0, dx, q], *late), dy, 0)

        def over_x(q):
            return tuple(piece[0, dx, q] for dx in range(1, n_w))

        def over_y(q):
            return tuple(piece[dy, 0, q] for dy in range(1, n_y))

        shares = []

        def share_of(target, choices, come=()):
            target = jnp.clip(target, 0, n_h - 1)
            owner, group = target // per_w, target % per_w
            dx, q = (w - owner) % n_w, slot_of(owner, group)
            picked = None
            for choice in choices:
                share = after(shares[choice], *come) if come else shares[choice]
                value = lax.dynamic_index_in_dim(share, dx, 0, keepdims=False)
                picked = value if picked is None else jnp.where(q == choice, value, picked)
            return picked.reshape(x_own.shape)

        def passes(targets):
            return sorted({slot(t // per_w, t % per_w) for t in targets})

        right, left, sums = [x_own], [x_own], [None, None]

        def step_planes(m, *late):
            step, apart = m - 1, n_h - m + 1
            to_right, to_left = (right[-1], left[-1]) if m < n_h else (None, None)
            if step:
                choices = passes([j + apart for j in range(step)] + [j - apart for j in range(apart, n_h)])
                come = tuple(sums)
                up, down = share_of(h + apart, choices, come), share_of(h - apart, choices, come)
                if step > 1:
                    up = (up.astype(jnp.float32) + sums[0].astype(jnp.float32)).astype(jnp.bfloat16)
                    down = (down.astype(jnp.float32) + sums[1].astype(jnp.float32)).astype(jnp.bfloat16)
                to_right = up if to_right is None else jnp.where(h >= step, to_right, up)
                to_left = down if to_left is None else jnp.where(h < apart, to_left, down)
            if late:
                to_right, to_left = after(to_right, *late), after(to_left, *late)
            come_right = lax.ppermute(to_right, "hidden", [(j, j + 1) for j in range(n_h - 1)])
            come_left = lax.ppermute(to_left, "hidden", [(j, j - 1) for j in range(1, n_h)])
            if m < n_h:
                right.append(come_right)
                left.append(come_left)
            sums[:] = [come_right, come_left]

        send_x(0)
        step_planes(1)
        send_y(0, *parts, *whole[1:])
        for dx in range(1, n_w):
            cores[0, dx, 0] = spread(piece[0, dx, 0])
        for q in range(per_w):
            late = tuple(shares[-1:])
            tokens = []
            for dx in range(n_w):
                for dc in range(n_c):
                    tokens.append((cores[0, dx, q][dc], w * 0) if dx else (whole[dc], slot_of(w, q)))
            due = late + tuple(parts)
            if q:
                due = late + (right[q], left[q]) + tuple(cores[dy, 0, q - 1][-1] for dy in range(1, n_y))
            if q + 1 < per_w:
                send_x(q + 1, *over_x(q), *whole[1:])
            share = input_grad(c, n_c, rows, tokens, weight, n_w, n_y, due)
            shares.append(share)
            for dy in range(1, n_y):
                cores[dy, 0, q] = spread(piece[dy, 0, q], share)
            if q + 1 < per_w:
                for dx in range(1, n_w):
                    cores[0, dx, q + 1] = spread(piece[0, dx, q + 1], share)
                step_planes(q + 2, *(cores[0, dx, q + 1][-1] for dx in range(1, n_w)))
                send_y(q + 1, share, *over_y(q))
                send_on(q, *over_x(q + 1))
        for q in range(per_w - 1, per_w):
            send_on(q, *over_y(q), *over_x(q), *shares[-1:])
        for dy in range(1, n_y):
            for dx in range(1, n_w):
                for q in range(per_w):
                    cores[dy, dx, q] = spread(piece[dy, dx, q])
        for m in range(per_w + 1, n_h):
            step_planes(m)
        due = tuple(sums)
        step_planes(n_h)

        places, pieces = [], []
        for k in range(n_h):
            if right[k] is left[k]:
                sides = [(jnp.where(h >= k, h - k, h + k), right[k], (h >= k) | (h + k < n_h))]
            else:
                sides = [(h - k, right[k], h >= k), (h + k, left[k], h + k < n_h)]
            for plane, planes_x, there in sides:
                owner, group = plane // per_w, plane % per_w
                dx = (w - owner) % n_w
                for dy in range(n_y):
                    sent_order = slot_of(owner, group) if dy else jnp.where(dx == 0, group, slot_of(owner, group))
                    place = jnp.where(there, dx * per_w + sent_order, -1).astype(jnp.int32)
                    places += [place] * n_c
                pieces.append(planes_x)
        s_pieces = []
        for dy in range(n_y):
            for dc in range(n_c):
                for dx in range(n_w):
                    if dy == dx == 0:
                        s_pieces.append(whole[dc])
                    else:
                        s_pieces += [cores[dy, dx, q][dc] for q in range(per_w)]
        places = jnp.stack(places)
        grad_weight = weight_grad(places, pieces, s_pieces, n_h, rows, due)
        from_left, from_right = after(sums[0], grad_weight), sums[1]
        total = share_of(h, range(per_w)).astype(jnp.float32)
        total = total + from_left.astype(jnp.float32) + from_right.astype(jnp.float32)
        total = total.astype(jnp.bfloat16).reshape(n_y, n_c, rows, d_own)
        held = [total[:, 0]] + [over_replica(total[:, dc], 0, n_c - dc) for dc in range(1, n_c)]
        held = jnp.stack(held)
        by_core = [lax.dynamic_index_in_dim(held, (p - c) % n_c, 0, keepdims=False) for p in range(n_c)]
        grad_input = jnp.concatenate([value[k] for value in by_core for k in range(n_y)], axis=1)
        return grad_input, grad_weight

    return body


def solution(mesh):
    in_specs = (
        P(("replica", "hidden"), "width"),
        P(("replica", "width"), "hidden"),
        P("width", "hidden"),
        P(),
        P(),
        P("replica"),
    )
    out_specs = (P(("replica", "hidden"), "width"), P(("width", "replica"), "hidden"))
    body = make_body(mesh.shape["hidden"], mesh.shape["width"], mesh.shape["replica"])
    return jax.shard_map(body, mesh=mesh, in_specs=in_specs, out_specs=out_specs, check_vma=False)
```

```python
import functools

import jax
import jax.numpy as jnp
from jax import lax
from jax.experimental import pallas as pl
from jax.experimental.pallas import tpu as pltpu
from jax.sharding import PartitionSpec as P

K = 4
CDW = 2
CDX = 0
VMEM = 60 << 20


def pass_weights(samples, correct):
    total = samples.astype(jnp.float32)
    good = correct.astype(jnp.float32)
    missing = jnp.ones_like(total)
    for factor_index in range(K):
        missing = missing * jnp.maximum(total - good - factor_index, 0.0) / (total - factor_index)
    return 1.0 - missing


def token_weights(prompt_ids, samples, correct):
    pass_at_k = pass_weights(samples, correct)
    prompt_range = jnp.arange(samples.shape[0], dtype=jnp.int32)
    matches = prompt_ids[:, None] == prompt_range[None, :]
    picked = jnp.sum(jnp.where(matches, pass_at_k[None, :], 0.0), axis=1, keepdims=True)
    rounded = lax.optimization_barrier(picked.astype(jnp.bfloat16))
    return rounded.astype(jnp.float32)


def COST_DW(m, f, tokens):
    return pl.CostEstimate(flops=CDW * m * f * tokens, bytes_accessed=CDW * (tokens * (m + f) + 2 * m * f), transcendentals=0)


def COST_DX(n, f, width):
    return pl.CostEstimate(flops=CDX * n * f * width, bytes_accessed=CDX * f * (width + n), transcendentals=0)


def after(value, *others):
    return lax.optimization_barrier((value,) + others)[0]


def weight_grad_kernel(place_ref, *refs, n_x, n_s, n_h, rows):
    x_refs, s_refs, out_ref, x_all, s_all = refs[:n_x], refs[n_x:n_x + n_s], refs[-3], refs[-2], refs[-1]
    groups = x_refs[0].shape[0] // rows

    @pl.when(pl.program_id(0) == 0)
    def _():
        for k in range(n_x):
            @pl.when(place_ref[k * groups] >= 0)
            def _(k=k):
                for g in range(groups):
                    start = pl.multiple_of((g * n_h + place_ref[k * groups + g]) * rows, rows)
                    x_all[pl.ds(start, rows), :] = x_refs[k][g * rows:(g + 1) * rows, :]

    start = 0
    for s_ref in s_refs:
        s_all[start:start + s_ref.shape[0], :] = s_ref[...]
        start += s_ref.shape[0]
    out_ref[...] = lax.dot_general(
        x_all[...], s_all[...], (((0,), (0,)), ((), ())), preferred_element_type=jnp.float32
    )


def column_block(f):
    return next((b for b in (1024, 512, 256, 128) if f % b == 0 and f // b > 2), f)


def weight_grad(places, x_pieces, s_pieces, n_h, rows, due):
    x_rows, m = x_pieces[0].shape
    f = s_pieces[0].shape[1]
    tokens = x_rows * n_h
    block = column_block(f)
    body = functools.partial(weight_grad_kernel, n_x=len(x_pieces), n_s=len(s_pieces), n_h=n_h, rows=rows)
    return pl.pallas_call(
        body,
        grid_spec=pltpu.PrefetchScalarGridSpec(
            num_scalar_prefetch=1,
            grid=(f // block,),
            in_specs=[pl.BlockSpec((x_rows, m), lambda j, p: (0, 0))] * len(x_pieces)
            + [pl.BlockSpec((piece.shape[0], block), lambda j, p: (0, j)) for piece in s_pieces],
            out_specs=pl.BlockSpec((m, block), lambda j, p: (0, j)),
            scratch_shapes=[pltpu.VMEM((tokens, m), jnp.bfloat16), pltpu.VMEM((tokens, block), jnp.bfloat16)],
        ),
        out_shape=jax.ShapeDtypeStruct((m, f), jnp.float32),
        compiler_params=pltpu.CompilerParams(vmem_limit_bytes=VMEM),
        cost_estimate=COST_DW(m, f, tokens),
    )(after(places, *due) if due else places, *x_pieces, *s_pieces)


def input_grad_kernel(first_ref, *refs):
    piece_refs, weight_ref, out_ref, tokens = refs[:-3], refs[-3], refs[-2], refs[-1]
    rows = piece_refs[0].shape[0]

    @pl.when(pl.program_id(0) == 0)
    def _():
        for k, piece_ref in enumerate(piece_refs):
            tokens[k * rows:(k + 1) * rows, :] = piece_ref[...]

    share = lax.dot_general(
        tokens[...], weight_ref[...], (((1,), (1,)), ((), ())), preferred_element_type=jnp.float32
    ).astype(out_ref.dtype)
    per_owner = out_ref.shape[2]
    for k in range(out_ref.shape[0]):
        out_ref[k, 0] = share[k * per_owner:(k + 1) * per_owner]


def input_grad(core, n_c, rows, pieces, weight, owners, parts, due):
    d, f = weight.shape
    width = d // n_c
    n = rows * len(pieces)
    part = width // parts
    block = next(b for b in (512, 256, 128, part) if part % b == 0)
    per_part = part // block
    steps = width // block
    first = jnp.stack([core * steps] + [index for _, index in pieces]).astype(jnp.int32)
    return pl.pallas_call(
        input_grad_kernel,
        grid_spec=pltpu.PrefetchScalarGridSpec(
            num_scalar_prefetch=1,
            grid=(steps,),
            in_specs=[pl.BlockSpec((rows, f), lambda j, c, k=k: (c[k + 1], 0)) for k in range(len(pieces))]
            + [pl.BlockSpec((block, f), lambda j, c: (c[0] + j, 0))],
            out_specs=pl.BlockSpec(
                (owners, 1, n // owners, block), lambda j, c: (0, j // per_part, 0, j % per_part)
            ),
            scratch_shapes=[pltpu.VMEM((n, f), jnp.bfloat16)],
        ),
        out_shape=jax.ShapeDtypeStruct((owners, parts, n // owners, part), jnp.bfloat16),
        compiler_params=pltpu.CompilerParams(vmem_limit_bytes=VMEM),
        cost_estimate=COST_DX(n, f, width),
    )(after(first, *due) if due else first, *[piece for piece, _ in pieces], weight)


def make_body(n_h, n_w, n_r):
    n_c = 2 if n_r % 2 == 0 else 1
    n_y = n_r // n_c
    per_w = n_h // n_w

    def slot(w_index, group):
        return group if w_index < n_w // 2 else per_w - 1 - group

    def slot_of(w_index, group):
        return jnp.where(w_index < n_w // 2, group, per_w - 1 - group)

    def replica_perm(dy, dc):
        return [
            (y * n_c + c, (y + dy) % n_y * n_c + (c + dc) % n_c) for y in range(n_y) for c in range(n_c)
        ]

    def over_replica(value, dy, dc):
        return lax.ppermute(value, "replica", replica_perm(dy, dc))

    def over_width(value, dx):
        return lax.ppermute(value, "width", [(w, (w + dx) % n_w) for w in range(n_w)])

    def body(saved_input, grad_out, weight, samples, correct, prompt_ids):
        h, w, r = lax.axis_index("hidden"), lax.axis_index("width"), lax.axis_index("replica")
        y, c = r // n_c, r % n_c
        x_rows, d_half = saved_input.shape
        s_rows, f = grad_out.shape
        rows = s_rows // per_w
        d_core = d_half // n_c
        d_own = d_half // n_r

        parts = []
        for dy in range(n_y):
            for dc in range(n_c):
                target = (y + dy) % n_y * n_c + (c + dc) % n_c
                part = lax.dynamic_slice_in_dim(saved_input, target * d_own, d_own, 1)
                parts.append(part if dy == dc == 0 else over_replica(part, dy, dc))
        x_own = jnp.concatenate(parts, axis=0)

        all_weights = token_weights(prompt_ids, samples, correct)
        scale = lax.dynamic_slice_in_dim(all_weights, w * s_rows, s_rows, 0)
        scaled = (grad_out.astype(jnp.float32) * scale).astype(jnp.bfloat16)

        own_group = [lax.dynamic_slice_in_dim(scaled, slot_of(w, q) * rows, rows, 0) for q in range(per_w)]

        def spread(value, *late):
            value = after(value, *late) if late else value
            return [value] + [over_replica(value, 0, dc) for dc in range(1, n_c)]

        whole = spread(scaled, *parts[1:n_c])
        x_own = after(x_own, *whole[1:])
        piece, cores = {}, {}

        def send_x(q, *late):
            own = after(own_group[q], *late) if late else own_group[q]
            for dx in range(1, n_w):
                piece[0, dx, q] = over_width(own, dx)

        def send_y(q, *late):
            own = after(own_group[q], *late)
            for dy in range(1, n_y):
                piece[dy, 0, q] = over_replica(own, dy, 0)

        def send_on(q, *late):
            for dy in range(1, n_y):
                for dx in range(1, n_w):
                    if q % 2 == 0:
                        piece[dy, dx, q] = over_width(after(piece[dy, 0, q], *late), dx)
                    else:
                        piece[dy, dx, q] = over_replica(after(piece[0, dx, q], *late), dy, 0)

        def over_x(q):
            return tuple(piece[0, dx, q] for dx in range(1, n_w))

        def over_y(q):
            return tuple(piece[dy, 0, q] for dy in range(1, n_y))

        shares = []

        def share_of(target, choices, come=()):
            target = jnp.clip(target, 0, n_h - 1)
            owner, group = target // per_w, target % per_w
            dx, q = (w - owner) % n_w, slot_of(owner, group)
            picked = None
            for choice in choices:
                share = after(shares[choice], *come) if come else shares[choice]
                value = lax.dynamic_index_in_dim(share, dx, 0, keepdims=False)
                picked = value if picked is None else jnp.where(q == choice, value, picked)
            return picked.reshape(x_own.shape)

        def passes(targets):
            return sorted({slot(t // per_w, t % per_w) for t in targets})

        even = h % 2 == 0
        pairs = [
            [edge for j in range(first, n_h - 1, 2) for edge in ((j, j + 1), (j + 1, j))] for first in range(2)
        ]
        planes = [(h, h >= 0, x_own)]
        came = [x_own, x_own]

        def step_planes(m, *late):
            step, apart = m - 1, n_h - m + 1
            choices = passes([j + apart for j in range(step)] + [j - apart for j in range(apart, n_h)]) if step else []
            come, sent = tuple(came), []
            for kind in range(2):
                to_right = even if kind == 0 else ~even
                value = come[1 - kind] if m < n_h else None
                if step:
                    total = share_of(jnp.where(to_right, h + apart, h - apart), choices, come)
                    if step > 1:
                        total = (total.astype(jnp.float32) + come[1 - kind].astype(jnp.float32)).astype(jnp.bfloat16)
                    is_input = jnp.where(to_right, h >= step, h < apart)
                    value = total if value is None else jnp.where(is_input, value, total)
                sent.append(after(value, *late) if late else value)
            for kind in range(2):
                came[kind] = lax.ppermute(sent[kind], "hidden", pairs[kind])
                from_right = even if kind == 0 else ~even
                if m < n_h:
                    plane = jnp.where(from_right, h + m, h - m)
                    planes.append((plane, (plane >= 0) & (plane < n_h), came[kind]))

        send_x(0)
        step_planes(1)
        came_in = [None, tuple(came)]
        send_y(0, *parts, *whole[1:])
        for dx in range(1, n_w):
            cores[0, dx, 0] = spread(piece[0, dx, 0])
        for q in range(per_w):
            late = tuple(shares[-1:])
            tokens = []
            for dx in range(n_w):
                for dc in range(n_c):
                    tokens.append((cores[0, dx, q][dc], w * 0) if dx else (whole[dc], slot_of(w, q)))
            due = late + tuple(parts)
            if q:
                due = late + tuple(came_in[q]) + tuple(cores[dy, 0, q - 1][-1] for dy in range(1, n_y))
            if q + 1 < per_w:
                send_x(q + 1, *over_x(q), *whole[1:])
            share = input_grad(c, n_c, rows, tokens, weight, n_w, n_y, due)
            shares.append(share)
            for dy in range(1, n_y):
                cores[dy, 0, q] = spread(piece[dy, 0, q], share)
            if q + 1 < per_w:
                for dx in range(1, n_w):
                    cores[0, dx, q + 1] = spread(piece[0, dx, q + 1], share)
                step_planes(q + 2, *(cores[0, dx, q + 1][-1] for dx in range(1, n_w)))
                came_in.append(tuple(came))
                send_y(q + 1, share, *over_y(q))
                send_on(q, *over_x(q + 1))
        for q in range(per_w - 1, per_w):
            send_on(q, *over_y(q), *over_x(q), *shares[-1:])
        for dy in range(1, n_y):
            for dx in range(1, n_w):
                for q in range(per_w):
                    cores[dy, dx, q] = spread(piece[dy, dx, q])
        for m in range(per_w + 1, n_h):
            step_planes(m)
        due = tuple(came)
        step_planes(n_h)

        places, pieces = [], []
        for plane, there, values in planes:
            owner, group = plane // per_w, plane % per_w
            dx = (w - owner) % n_w
            for dy in range(n_y):
                sent_order = slot_of(owner, group) if dy else jnp.where(dx == 0, group, slot_of(owner, group))
                place = jnp.where(there, dx * per_w + sent_order, -1).astype(jnp.int32)
                places += [place] * n_c
            pieces.append(values)
        s_pieces = []
        for dy in range(n_y):
            for dc in range(n_c):
                for dx in range(n_w):
                    if dy == dx == 0:
                        s_pieces.append(whole[dc])
                    else:
                        s_pieces += [cores[dy, dx, q][dc] for q in range(per_w)]
        places = jnp.stack(places)
        grad_weight = weight_grad(places, pieces, s_pieces, n_h, rows, due)
        came[0] = after(came[0], grad_weight)
        total = share_of(h, range(per_w)).astype(jnp.float32)
        total = total + came[0].astype(jnp.float32) + came[1].astype(jnp.float32)
        total = total.astype(jnp.bfloat16).reshape(n_y, n_c, rows, d_own)
        held = [total[:, 0]] + [over_replica(total[:, dc], 0, n_c - dc) for dc in range(1, n_c)]
        held = jnp.stack(held)
        by_core = [lax.dynamic_index_in_dim(held, (p - c) % n_c, 0, keepdims=False) for p in range(n_c)]
        grad_input = jnp.concatenate([value[k] for value in by_core for k in range(n_y)], axis=1)
        return grad_input, grad_weight

    return body


def solution(mesh):
    in_specs = (
        P(("replica", "hidden"), "width"),
        P(("replica", "width"), "hidden"),
        P("width", "hidden"),
        P(),
        P(),
        P("replica"),
    )
    out_specs = (P(("replica", "hidden"), "width"), P(("width", "replica"), "hidden"))
    body = make_body(mesh.shape["hidden"], mesh.shape["width"], mesh.shape["replica"])
    return jax.shard_map(body, mesh=mesh, in_specs=in_specs, out_specs=out_specs, check_vma=False)
```

```python
import functools

import jax
import jax.numpy as jnp
from jax import lax
from jax.experimental import pallas as pl
from jax.experimental.pallas import tpu as pltpu
from jax.sharding import PartitionSpec as P

K = 4
CDW = 2
CDX = 0
VMEM = 60 << 20


def pass_weights(samples, correct):
    total = samples.astype(jnp.float32)
    good = correct.astype(jnp.float32)
    missing = jnp.ones_like(total)
    for factor_index in range(K):
        missing = missing * jnp.maximum(total - good - factor_index, 0.0) / (total - factor_index)
    return 1.0 - missing


def token_weights(prompt_ids, samples, correct):
    pass_at_k = pass_weights(samples, correct)
    prompt_range = jnp.arange(samples.shape[0], dtype=jnp.int32)
    matches = prompt_ids[:, None] == prompt_range[None, :]
    picked = jnp.sum(jnp.where(matches, pass_at_k[None, :], 0.0), axis=1, keepdims=True)
    rounded = lax.optimization_barrier(picked.astype(jnp.bfloat16))
    return rounded.astype(jnp.float32)


def COST_DW(m, f, tokens):
    return pl.CostEstimate(flops=CDW * m * f * tokens, bytes_accessed=CDW * (tokens * (m + f) + 2 * m * f), transcendentals=0)


def COST_DX(n, f, width):
    return pl.CostEstimate(flops=CDX * n * f * width, bytes_accessed=CDX * f * (width + n), transcendentals=0)


def after(value, *others):
    return lax.optimization_barrier((value,) + others)[0]


def weight_grad_kernel(place_ref, *refs, n_x, n_s, n_h, rows):
    x_refs, s_refs, out_ref, x_all, s_all = refs[:n_x], refs[n_x:n_x + n_s], refs[-3], refs[-2], refs[-1]
    groups = x_refs[0].shape[0] // rows

    @pl.when(pl.program_id(0) == 0)
    def _():
        for k in range(n_x):
            @pl.when(place_ref[k * groups] >= 0)
            def _(k=k):
                for g in range(groups):
                    start = pl.multiple_of((g * n_h + place_ref[k * groups + g]) * rows, rows)
                    x_all[pl.ds(start, rows), :] = x_refs[k][g * rows:(g + 1) * rows, :]

    start = 0
    for s_ref in s_refs:
        s_all[start:start + s_ref.shape[0], :] = s_ref[...]
        start += s_ref.shape[0]
    out_ref[...] = lax.dot_general(
        x_all[...], s_all[...], (((0,), (0,)), ((), ())), preferred_element_type=jnp.float32
    )


def column_block(f):
    return next((b for b in (1024, 512, 256, 128) if f % b == 0 and f // b > 2), f)


def weight_grad(places, x_pieces, s_pieces, n_h, rows, due):
    x_rows, m = x_pieces[0].shape
    f = s_pieces[0].shape[1]
    tokens = x_rows * n_h
    block = column_block(f)
    body = functools.partial(weight_grad_kernel, n_x=len(x_pieces), n_s=len(s_pieces), n_h=n_h, rows=rows)
    return pl.pallas_call(
        body,
        grid_spec=pltpu.PrefetchScalarGridSpec(
            num_scalar_prefetch=1,
            grid=(f // block,),
            in_specs=[pl.BlockSpec((x_rows, m), lambda j, p: (0, 0))] * len(x_pieces)
            + [pl.BlockSpec((piece.shape[0], block), lambda j, p: (0, j)) for piece in s_pieces],
            out_specs=pl.BlockSpec((m, block), lambda j, p: (0, j)),
            scratch_shapes=[pltpu.VMEM((tokens, m), jnp.bfloat16), pltpu.VMEM((tokens, block), jnp.bfloat16)],
        ),
        out_shape=jax.ShapeDtypeStruct((m, f), jnp.float32),
        compiler_params=pltpu.CompilerParams(vmem_limit_bytes=VMEM),
        cost_estimate=COST_DW(m, f, tokens),
    )(after(places, *due) if due else places, *x_pieces, *s_pieces)


def input_grad_kernel(first_ref, *refs):
    piece_refs, weight_ref, out_ref, tokens = refs[:-3], refs[-3], refs[-2], refs[-1]
    rows = piece_refs[0].shape[0]

    @pl.when(pl.program_id(0) == 0)
    def _():
        for k, piece_ref in enumerate(piece_refs):
            tokens[k * rows:(k + 1) * rows, :] = piece_ref[...]

    share = lax.dot_general(
        tokens[...], weight_ref[...], (((1,), (1,)), ((), ())), preferred_element_type=jnp.float32
    ).astype(out_ref.dtype)
    per_owner = out_ref.shape[2]
    for k in range(out_ref.shape[0]):
        out_ref[k, 0] = share[k * per_owner:(k + 1) * per_owner]


def input_grad(core, n_c, rows, pieces, weight, owners, parts, due):
    d, f = weight.shape
    width = d // n_c
    n = rows * len(pieces)
    part = width // parts
    block = next(b for b in (512, 256, 128, part) if part % b == 0)
    per_part = part // block
    steps = width // block
    first = jnp.stack([core * steps] + [index for _, index in pieces]).astype(jnp.int32)
    return pl.pallas_call(
        input_grad_kernel,
        grid_spec=pltpu.PrefetchScalarGridSpec(
            num_scalar_prefetch=1,
            grid=(steps,),
            in_specs=[pl.BlockSpec((rows, f), lambda j, c, k=k: (c[k + 1], 0)) for k in range(len(pieces))]
            + [pl.BlockSpec((block, f), lambda j, c: (c[0] + j, 0))],
            out_specs=pl.BlockSpec(
                (owners, 1, n // owners, block), lambda j, c: (0, j // per_part, 0, j % per_part)
            ),
            scratch_shapes=[pltpu.VMEM((n, f), jnp.bfloat16)],
        ),
        out_shape=jax.ShapeDtypeStruct((owners, parts, n // owners, part), jnp.bfloat16),
        compiler_params=pltpu.CompilerParams(vmem_limit_bytes=VMEM),
        cost_estimate=COST_DX(n, f, width),
    )(after(first, *due) if due else first, *[piece for piece, _ in pieces], weight)


def step_kernel(pick_ref, *refs, choices, has_input, has_sum):
    n = len(choices)
    come_refs, share_refs, out_refs = refs[:-2 * n - 2], refs[-2 * n - 2:-2], refs[-2:]
    for kind in range(2):
        dx, q, is_input = (pick_ref[3 * kind + i] for i in range(3))
        out_ref = out_refs[kind]
        if has_input:
            @pl.when(is_input == 1)
            def _(kind=kind, out_ref=out_ref):
                out_ref[...] = come_refs[1 - kind][...]

        for i, choice in enumerate(choices):
            @pl.when((is_input == 0) & (q == choice))
            def _(kind=kind, out_ref=out_ref, i=i):
                share = share_refs[n * kind + i][0, 0]
                if has_sum:
                    share = share.astype(jnp.float32) + come_refs[1 - kind][...].astype(jnp.float32)
                out_ref[...] = share.astype(out_ref.dtype)


def step_values(picks, come, shares, choices, has_input, has_sum):
    _, n_y, rows, columns = shares[0].shape
    block = next((b for b in (768, 512, 384, 256, 128) if columns % b == 0), columns)
    flat = pl.BlockSpec((rows, block), lambda y, j, p: (y, j))
    return pl.pallas_call(
        functools.partial(step_kernel, choices=choices, has_input=has_input, has_sum=has_sum),
        grid_spec=pltpu.PrefetchScalarGridSpec(
            num_scalar_prefetch=1,
            grid=(n_y, columns // block),
            in_specs=[flat] * len(come)
            + [
                pl.BlockSpec((1, 1, rows, block), lambda y, j, p, kind=kind: (p[3 * kind], y, 0, j))
                for kind in range(2)
                for _ in choices
            ],
            out_specs=[flat, flat],
        ),
        out_shape=[jax.ShapeDtypeStruct((n_y * rows, columns), jnp.bfloat16)] * 2,
        compiler_params=pltpu.CompilerParams(vmem_limit_bytes=VMEM),
    )(picks, *come, *(shares[choice] for choice in choices * 2))


def make_body(n_h, n_w, n_r):
    n_c = 2 if n_r % 2 == 0 else 1
    n_y = n_r // n_c
    per_w = n_h // n_w

    def slot(w_index, group):
        return group if w_index < n_w // 2 else per_w - 1 - group

    def slot_of(w_index, group):
        return jnp.where(w_index < n_w // 2, group, per_w - 1 - group)

    def replica_perm(dy, dc):
        return [
            (y * n_c + c, (y + dy) % n_y * n_c + (c + dc) % n_c) for y in range(n_y) for c in range(n_c)
        ]

    def over_replica(value, dy, dc):
        return lax.ppermute(value, "replica", replica_perm(dy, dc))

    def over_width(value, dx):
        return lax.ppermute(value, "width", [(w, (w + dx) % n_w) for w in range(n_w)])

    def body(saved_input, grad_out, weight, samples, correct, prompt_ids):
        h, w, r = lax.axis_index("hidden"), lax.axis_index("width"), lax.axis_index("replica")
        y, c = r // n_c, r % n_c
        x_rows, d_half = saved_input.shape
        s_rows, f = grad_out.shape
        rows = s_rows // per_w
        d_core = d_half // n_c
        d_own = d_half // n_r

        parts = []
        for dy in range(n_y):
            for dc in range(n_c):
                target = (y + dy) % n_y * n_c + (c + dc) % n_c
                part = lax.dynamic_slice_in_dim(saved_input, target * d_own, d_own, 1)
                parts.append(part if dy == dc == 0 else over_replica(part, dy, dc))
        x_own = jnp.concatenate(parts, axis=0)

        all_weights = token_weights(prompt_ids, samples, correct)
        scale = lax.dynamic_slice_in_dim(all_weights, w * s_rows, s_rows, 0)
        scaled = (grad_out.astype(jnp.float32) * scale).astype(jnp.bfloat16)

        own_group = [lax.dynamic_slice_in_dim(scaled, slot_of(w, q) * rows, rows, 0) for q in range(per_w)]

        def spread(value, *late):
            value = after(value, *late) if late else value
            return [value] + [over_replica(value, 0, dc) for dc in range(1, n_c)]

        whole = spread(scaled, *parts[1:n_c])
        x_own = after(x_own, *whole[1:])
        piece, cores = {}, {}

        def send_x(q, *late):
            own = after(own_group[q], *late) if late else own_group[q]
            for dx in range(1, n_w):
                piece[0, dx, q] = over_width(own, dx)

        def send_y(q, *late):
            own = after(own_group[q], *late)
            for dy in range(1, n_y):
                piece[dy, 0, q] = over_replica(own, dy, 0)

        def send_on(q, *late):
            for dy in range(1, n_y):
                for dx in range(1, n_w):
                    if q % 2 == 0:
                        piece[dy, dx, q] = over_width(after(piece[dy, 0, q], *late), dx)
                    else:
                        piece[dy, dx, q] = over_replica(after(piece[0, dx, q], *late), dy, 0)

        def over_x(q):
            return tuple(piece[0, dx, q] for dx in range(1, n_w))

        def over_y(q):
            return tuple(piece[dy, 0, q] for dy in range(1, n_y))

        shares = []

        def share_of(target, choices, come=()):
            target = jnp.clip(target, 0, n_h - 1)
            owner, group = target // per_w, target % per_w
            dx, q = (w - owner) % n_w, slot_of(owner, group)
            picked = None
            for choice in choices:
                share = after(shares[choice], *come) if come else shares[choice]
                value = lax.dynamic_index_in_dim(share, dx, 0, keepdims=False)
                picked = value if picked is None else jnp.where(q == choice, value, picked)
            return picked.reshape(x_own.shape)

        def passes(targets):
            return sorted({slot(t // per_w, t % per_w) for t in targets})

        even = h % 2 == 0
        pairs = [
            [edge for j in range(first, n_h - 1, 2) for edge in ((j, j + 1), (j + 1, j))] for first in range(2)
        ]
        planes = [(h, h >= 0, x_own)]
        came = [x_own, x_own]

        def step_planes(m, *late):
            step, apart = m - 1, n_h - m + 1
            choices = passes([j + apart for j in range(step)] + [j - apart for j in range(apart, n_h)]) if step else []
            come, picks = tuple(came), []
            for kind in range(2):
                to_right = even if kind == 0 else ~even
                target = jnp.clip(jnp.where(to_right, h + apart, h - apart), 0, n_h - 1)
                owner, group = target // per_w, target % per_w
                is_input = jnp.where(to_right, h >= step, h < apart) & (m < n_h)
                picks += [(w - owner) % n_w, slot_of(owner, group), is_input.astype(jnp.int32)]
            if step:
                picks = jnp.stack(picks).astype(jnp.int32)
                sent = step_values(picks, come, shares, choices, m < n_h, step > 1)
            else:
                sent = [come[1], come[0]]
            if late:
                sent = [after(value, *late) for value in sent]
            for kind in range(2):
                came[kind] = lax.ppermute(sent[kind], "hidden", pairs[kind])
                from_right = even if kind == 0 else ~even
                if m < n_h:
                    plane = jnp.where(from_right, h + m, h - m)
                    planes.append((plane, (plane >= 0) & (plane < n_h), came[kind]))

        send_x(0)
        step_planes(1)
        came_in = [None, tuple(came)]
        send_y(0, *parts, *whole[1:])
        for dx in range(1, n_w):
            cores[0, dx, 0] = spread(piece[0, dx, 0])
        for q in range(per_w):
            late = tuple(shares[-1:])
            tokens = []
            for dx in range(n_w):
                for dc in range(n_c):
                    tokens.append((cores[0, dx, q][dc], w * 0) if dx else (whole[dc], slot_of(w, q)))
            due = late + tuple(parts)
            if q:
                due = late + tuple(came_in[q]) + tuple(cores[dy, 0, q - 1][-1] for dy in range(1, n_y))
            if q + 1 < per_w:
                send_x(q + 1, *over_x(q), *whole[1:])
            share = input_grad(c, n_c, rows, tokens, weight, n_w, n_y, due)
            shares.append(share)
            for dy in range(1, n_y):
                cores[dy, 0, q] = spread(piece[dy, 0, q], share)
            if q + 1 < per_w:
                for dx in range(1, n_w):
                    cores[0, dx, q + 1] = spread(piece[0, dx, q + 1], share)
                step_planes(q + 2, *(cores[0, dx, q + 1][-1] for dx in range(1, n_w)))
                came_in.append(tuple(came))
                send_y(q + 1, share, *over_y(q))
                send_on(q, *over_x(q + 1))
        for q in range(per_w - 1, per_w):
            send_on(q, *over_y(q), *over_x(q), *shares[-1:])
        for dy in range(1, n_y):
            for dx in range(1, n_w):
                for q in range(per_w):
                    cores[dy, dx, q] = spread(piece[dy, dx, q])
        for m in range(per_w + 1, n_h):
            step_planes(m)
        due = tuple(came)
        step_planes(n_h)

        places, pieces = [], []
        for plane, there, values in planes:
            owner, group = plane // per_w, plane % per_w
            dx = (w - owner) % n_w
            for dy in range(n_y):
                sent_order = slot_of(owner, group) if dy else jnp.where(dx == 0, group, slot_of(owner, group))
                place = jnp.where(there, dx * per_w + sent_order, -1).astype(jnp.int32)
                places += [place] * n_c
            pieces.append(values)
        s_pieces = []
        for dy in range(n_y):
            for dc in range(n_c):
                for dx in range(n_w):
                    if dy == dx == 0:
                        s_pieces.append(whole[dc])
                    else:
                        s_pieces += [cores[dy, dx, q][dc] for q in range(per_w)]
        places = jnp.stack(places)
        grad_weight = weight_grad(places, pieces, s_pieces, n_h, rows, due)
        came[0] = after(came[0], grad_weight)
        total = share_of(h, range(per_w)).astype(jnp.float32)
        total = total + came[0].astype(jnp.float32) + came[1].astype(jnp.float32)
        total = total.astype(jnp.bfloat16).reshape(n_y, n_c, rows, d_own)
        held = [total[:, 0]] + [over_replica(total[:, dc], 0, n_c - dc) for dc in range(1, n_c)]
        held = jnp.stack(held)
        by_core = [lax.dynamic_index_in_dim(held, (p - c) % n_c, 0, keepdims=False) for p in range(n_c)]
        grad_input = jnp.concatenate([value[k] for value in by_core for k in range(n_y)], axis=1)
        return grad_input, grad_weight

    return body


def solution(mesh):
    in_specs = (
        P(("replica", "hidden"), "width"),
        P(("replica", "width"), "hidden"),
        P("width", "hidden"),
        P(),
        P(),
        P("replica"),
    )
    out_specs = (P(("replica", "hidden"), "width"), P(("width", "replica"), "hidden"))
    body = make_body(mesh.shape["hidden"], mesh.shape["width"], mesh.shape["replica"])
    return jax.shard_map(body, mesh=mesh, in_specs=in_specs, out_specs=out_specs, check_vma=False)
```

```python
import functools

import jax
import jax.numpy as jnp
from jax import lax
from jax.experimental import pallas as pl
from jax.experimental.pallas import tpu as pltpu
from jax.sharding import PartitionSpec as P

K = 4
CDW = 2
CDX = 0
VMEM = 60 << 20


def pass_weights(samples, correct):
    total = samples.astype(jnp.float32)
    good = correct.astype(jnp.float32)
    missing = jnp.ones_like(total)
    for factor_index in range(K):
        missing = missing * jnp.maximum(total - good - factor_index, 0.0) / (total - factor_index)
    return 1.0 - missing


def token_weights(prompt_ids, samples, correct):
    pass_at_k = pass_weights(samples, correct)
    prompt_range = jnp.arange(samples.shape[0], dtype=jnp.int32)
    matches = prompt_ids[:, None] == prompt_range[None, :]
    picked = jnp.sum(jnp.where(matches, pass_at_k[None, :], 0.0), axis=1, keepdims=True)
    rounded = lax.optimization_barrier(picked.astype(jnp.bfloat16))
    return rounded.astype(jnp.float32)


def COST_DW(m, f, tokens):
    return pl.CostEstimate(flops=CDW * m * f * tokens, bytes_accessed=CDW * (tokens * (m + f) + 2 * m * f), transcendentals=0)


def COST_DX(n, f, width):
    return pl.CostEstimate(flops=CDX * n * f * width, bytes_accessed=CDX * f * (width + n), transcendentals=0)


def after(value, *others):
    return lax.optimization_barrier((value,) + others)[0]


def weight_grad_kernel(place_ref, *refs, n_x, n_s, n_h, rows):
    x_refs, s_refs, out_ref, x_all, s_all = refs[:n_x], refs[n_x:n_x + n_s], refs[-3], refs[-2], refs[-1]
    groups = x_refs[0].shape[0] // rows

    @pl.when(pl.program_id(0) == 0)
    def _():
        for k in range(n_x):
            @pl.when(place_ref[k * groups] >= 0)
            def _(k=k):
                for g in range(groups):
                    start = pl.multiple_of((g * n_h + place_ref[k * groups + g]) * rows, rows)
                    x_all[pl.ds(start, rows), :] = x_refs[k][g * rows:(g + 1) * rows, :]

    start = 0
    for s_ref in s_refs:
        s_all[start:start + s_ref.shape[0], :] = s_ref[...]
        start += s_ref.shape[0]
    out_ref[...] = lax.dot_general(
        x_all[...], s_all[...], (((0,), (0,)), ((), ())), preferred_element_type=jnp.float32
    )


def column_block(f):
    return next((b for b in (1024, 512, 256, 128) if f % b == 0 and f // b > 2), f)


def weight_grad(places, x_pieces, s_pieces, n_h, rows, due):
    x_rows, m = x_pieces[0].shape
    f = s_pieces[0].shape[1]
    tokens = x_rows * n_h
    block = column_block(f)
    body = functools.partial(weight_grad_kernel, n_x=len(x_pieces), n_s=len(s_pieces), n_h=n_h, rows=rows)
    return pl.pallas_call(
        body,
        grid_spec=pltpu.PrefetchScalarGridSpec(
            num_scalar_prefetch=1,
            grid=(f // block,),
            in_specs=[pl.BlockSpec((x_rows, m), lambda j, p: (0, 0))] * len(x_pieces)
            + [pl.BlockSpec((piece.shape[0], block), lambda j, p: (0, j)) for piece in s_pieces],
            out_specs=pl.BlockSpec((m, block), lambda j, p: (0, j)),
            scratch_shapes=[pltpu.VMEM((tokens, m), jnp.bfloat16), pltpu.VMEM((tokens, block), jnp.bfloat16)],
        ),
        out_shape=jax.ShapeDtypeStruct((m, f), jnp.float32),
        compiler_params=pltpu.CompilerParams(vmem_limit_bytes=VMEM),
        cost_estimate=COST_DW(m, f, tokens),
    )(after(places, *due) if due else places, *x_pieces, *s_pieces)


def input_grad_kernel(first_ref, *refs):
    piece_refs, weight_ref, out_ref, tokens = refs[:-3], refs[-3], refs[-2], refs[-1]
    rows = piece_refs[0].shape[0]

    @pl.when(pl.program_id(0) == 0)
    def _():
        for k, piece_ref in enumerate(piece_refs):
            tokens[k * rows:(k + 1) * rows, :] = piece_ref[...]

    share = lax.dot_general(
        tokens[...], weight_ref[...], (((1,), (1,)), ((), ())), preferred_element_type=jnp.float32
    ).astype(out_ref.dtype)
    per_owner = out_ref.shape[2]
    for k in range(out_ref.shape[0]):
        out_ref[k, 0] = share[k * per_owner:(k + 1) * per_owner]


def input_grad(core, n_c, rows, pieces, weight, owners, parts, due):
    d, f = weight.shape
    width = d // n_c
    n = rows * len(pieces)
    part = width // parts
    block = next(b for b in (512, 256, 128, part) if part % b == 0)
    per_part = part // block
    steps = width // block
    first = jnp.stack([core * steps] + [index for _, index in pieces]).astype(jnp.int32)
    return pl.pallas_call(
        input_grad_kernel,
        grid_spec=pltpu.PrefetchScalarGridSpec(
            num_scalar_prefetch=1,
            grid=(steps,),
            in_specs=[pl.BlockSpec((rows, f), lambda j, c, k=k: (c[k + 1], 0)) for k in range(len(pieces))]
            + [pl.BlockSpec((block, f), lambda j, c: (c[0] + j, 0))],
            out_specs=pl.BlockSpec(
                (owners, 1, n // owners, block), lambda j, c: (0, j // per_part, 0, j % per_part)
            ),
            scratch_shapes=[pltpu.VMEM((n, f), jnp.bfloat16)],
        ),
        out_shape=jax.ShapeDtypeStruct((owners, parts, n // owners, part), jnp.bfloat16),
        compiler_params=pltpu.CompilerParams(vmem_limit_bytes=VMEM),
        cost_estimate=COST_DX(n, f, width),
    )(after(first, *due) if due else first, *[piece for piece, _ in pieces], weight)


def make_body(n_h, n_w, n_r):
    n_c = 2 if n_r % 2 == 0 else 1
    n_y = n_r // n_c
    per_w = n_h // n_w

    def slot(w_index, group):
        return group if w_index < n_w // 2 else per_w - 1 - group

    def slot_of(w_index, group):
        return jnp.where(w_index < n_w // 2, group, per_w - 1 - group)

    def replica_perm(dy, dc):
        return [
            (y * n_c + c, (y + dy) % n_y * n_c + (c + dc) % n_c) for y in range(n_y) for c in range(n_c)
        ]

    def over_replica(value, dy, dc):
        return lax.ppermute(value, "replica", replica_perm(dy, dc))

    def over_width(value, dx):
        return lax.ppermute(value, "width", [(w, (w + dx) % n_w) for w in range(n_w)])

    def body(saved_input, grad_out, weight, samples, correct, prompt_ids):
        h, w, r = lax.axis_index("hidden"), lax.axis_index("width"), lax.axis_index("replica")
        y, c = r // n_c, r % n_c
        x_rows, d_half = saved_input.shape
        s_rows, f = grad_out.shape
        rows = s_rows // per_w
        d_core = d_half // n_c
        d_own = d_half // n_r

        parts = []
        for dy in range(n_y):
            for dc in range(n_c):
                target = (y + dy) % n_y * n_c + (c + dc) % n_c
                part = lax.dynamic_slice_in_dim(saved_input, target * d_own, d_own, 1)
                parts.append(part if dy == dc == 0 else over_replica(part, dy, dc))
        x_own = jnp.concatenate(parts, axis=0)

        all_weights = token_weights(prompt_ids, samples, correct)
        scale = lax.dynamic_slice_in_dim(all_weights, w * s_rows, s_rows, 0)
        scaled = (grad_out.astype(jnp.float32) * scale).astype(jnp.bfloat16)

        own_group = [lax.dynamic_slice_in_dim(scaled, slot_of(w, q) * rows, rows, 0) for q in range(per_w)]

        def spread(value, *late):
            value = after(value, *late) if late else value
            return [value] + [over_replica(value, 0, dc) for dc in range(1, n_c)]

        whole = spread(scaled)
        piece, cores = {}, {}

        def send_x(q, *late):
            own = after(own_group[q], *late) if late else own_group[q]
            for dx in range(1, n_w):
                piece[0, dx, q] = over_width(own, dx)

        def send_y(q, *late):
            own = after(own_group[q], *late)
            for dy in range(1, n_y):
                piece[dy, 0, q] = over_replica(own, dy, 0)

        def send_on(q, *late):
            for dy in range(1, n_y):
                for dx in range(1, n_w):
                    if q % 2 == 0:
                        piece[dy, dx, q] = over_width(after(piece[dy, 0, q], *late), dx)
                    else:
                        piece[dy, dx, q] = over_replica(after(piece[0, dx, q], *late), dy, 0)

        def over_x(q):
            return tuple(piece[0, dx, q] for dx in range(1, n_w))

        def over_y(q):
            return tuple(piece[dy, 0, q] for dy in range(1, n_y))

        shares = []

        def share_of(target, choices, come=()):
            target = jnp.clip(target, 0, n_h - 1)
            owner, group = target // per_w, target % per_w
            dx, q = (w - owner) % n_w, slot_of(owner, group)
            picked = None
            for choice in choices:
                share = after(shares[choice], *come) if come else shares[choice]
                value = lax.dynamic_index_in_dim(share, dx, 0, keepdims=False)
                picked = value if picked is None else jnp.where(q == choice, value, picked)
            return picked.reshape(x_own.shape)

        def passes(targets):
            return sorted({slot(t // per_w, t % per_w) for t in targets})

        even = h % 2 == 0
        pairs = [
            [edge for j in range(first, n_h - 1, 2) for edge in ((j, j + 1), (j + 1, j))] for first in range(2)
        ]
        planes = [(h, h >= 0, x_own)]
        came = [x_own, x_own]

        def step_planes(m, *late):
            step, apart = m - 1, n_h - m + 1
            choices = passes([j + apart for j in range(step)] + [j - apart for j in range(apart, n_h)]) if step else []
            come, sent = tuple(came), []
            for kind in range(2):
                to_right = even if kind == 0 else ~even
                value = come[1 - kind] if m < n_h else None
                if step:
                    total = share_of(jnp.where(to_right, h + apart, h - apart), choices, come)
                    if step > 1:
                        total = (total.astype(jnp.float32) + come[1 - kind].astype(jnp.float32)).astype(jnp.bfloat16)
                    is_input = jnp.where(to_right, h >= step, h < apart)
                    value = total if value is None else jnp.where(is_input, value, total)
                sent.append(after(value, *late) if late else value)
            for kind in range(2):
                came[kind] = lax.ppermute(sent[kind], "hidden", pairs[kind])
                from_right = even if kind == 0 else ~even
                if m < n_h:
                    plane = jnp.where(from_right, h + m, h - m)
                    planes.append((plane, (plane >= 0) & (plane < n_h), came[kind]))

        send_x(0)
        step_planes(1)
        came_in = [None, tuple(came)]
        send_y(0, *parts, *whole[1:])
        cut = rows // 2 if rows % 32 == 0 else rows
        for dx in range(1, n_w):
            cores[0, dx, 0] = [piece[0, dx, 0]] + [
                [over_replica(piece[0, dx, 0][i:i + cut], 0, dc) for i in range(0, rows, cut)] for dc in range(1, n_c)
            ]
        for q in range(per_w):
            late = tuple(shares[-1:])
            tokens = []
            for dx in range(n_w):
                for dc in range(n_c):
                    held = cores[0, dx, q][dc] if dx else None
                    for i in range(rows // cut):
                        if not dx:
                            tokens.append((whole[dc], slot_of(w, q) * (rows // cut) + i))
                        elif isinstance(held, list):
                            tokens.append((held[i], w * 0))
                        else:
                            tokens.append((held, w * 0 + i))
            due = late + tuple(parts)
            if q:
                due = late + tuple(came_in[q]) + tuple(cores[dy, 0, q - 1][-1] for dy in range(1, n_y))
            if q + 1 < per_w:
                send_x(q + 1, *whole[1:])
            share = input_grad(c, n_c, cut, tokens, weight, n_w, n_y, due)
            shares.append(share)
            for dy in range(1, n_y):
                cores[dy, 0, q] = spread(piece[dy, 0, q], share)
            if q + 1 < per_w:
                for dx in range(1, n_w):
                    cores[0, dx, q + 1] = spread(piece[0, dx, q + 1], share)
                step_planes(q + 2, *(cores[0, dx, q + 1][-1] for dx in range(1, n_w)))
                came_in.append(tuple(came))
                send_y(q + 1, share, *over_y(q))
                send_on(q, *over_x(q + 1))
        for q in range(per_w - 1, per_w):
            send_on(q, *over_y(q), *over_x(q), *shares[-1:])
        for dy in range(1, n_y):
            for dx in range(1, n_w):
                for q in range(per_w):
                    cores[dy, dx, q] = spread(piece[dy, dx, q])
        for m in range(per_w + 1, n_h):
            step_planes(m)
        due = tuple(came)
        step_planes(n_h)

        places, pieces = [], []
        for plane, there, values in planes:
            owner, group = plane // per_w, plane % per_w
            dx = (w - owner) % n_w
            for dy in range(n_y):
                sent_order = slot_of(owner, group) if dy else jnp.where(dx == 0, group, slot_of(owner, group))
                place = jnp.where(there, dx * per_w + sent_order, -1).astype(jnp.int32)
                places += [place] * n_c
            pieces.append(values)
        s_pieces = []
        for dy in range(n_y):
            for dc in range(n_c):
                for dx in range(n_w):
                    if dy == dx == 0:
                        s_pieces.append(whole[dc])
                    else:
                        for q in range(per_w):
                            held = cores[dy, dx, q][dc]
                            s_pieces += held if isinstance(held, list) else [held]
        places = jnp.stack(places)
        grad_weight = weight_grad(places, pieces, s_pieces, n_h, rows, due)
        came[0] = after(came[0], grad_weight)
        total = share_of(h, range(per_w)).astype(jnp.float32)
        total = total + came[0].astype(jnp.float32) + came[1].astype(jnp.float32)
        total = total.astype(jnp.bfloat16).reshape(n_y, n_c, rows, d_own)
        held = [total[:, 0]] + [over_replica(total[:, dc], 0, n_c - dc) for dc in range(1, n_c)]
        held = jnp.stack(held)
        by_core = [lax.dynamic_index_in_dim(held, (p - c) % n_c, 0, keepdims=False) for p in range(n_c)]
        grad_input = jnp.concatenate([value[k] for value in by_core for k in range(n_y)], axis=1)
        return grad_input, grad_weight

    return body


def solution(mesh):
    in_specs = (
        P(("replica", "hidden"), "width"),
        P(("replica", "width"), "hidden"),
        P("width", "hidden"),
        P(),
        P(),
        P("replica"),
    )
    out_specs = (P(("replica", "hidden"), "width"), P(("width", "replica"), "hidden"))
    body = make_body(mesh.shape["hidden"], mesh.shape["width"], mesh.shape["replica"])
    return jax.shard_map(body, mesh=mesh, in_specs=in_specs, out_specs=out_specs, check_vma=False)
```

```python
import functools

import jax
import jax.numpy as jnp
from jax import lax
from jax.experimental import pallas as pl
from jax.experimental.pallas import tpu as pltpu
from jax.sharding import PartitionSpec as P

K = 4
CDW = 2
CDX = 0
VMEM = 60 << 20


def pass_weights(samples, correct):
    total = samples.astype(jnp.float32)
    good = correct.astype(jnp.float32)
    missing = jnp.ones_like(total)
    for factor_index in range(K):
        missing = missing * jnp.maximum(total - good - factor_index, 0.0) / (total - factor_index)
    return 1.0 - missing


def token_weights(prompt_ids, samples, correct):
    pass_at_k = pass_weights(samples, correct)
    prompt_range = jnp.arange(samples.shape[0], dtype=jnp.int32)
    matches = prompt_ids[:, None] == prompt_range[None, :]
    picked = jnp.sum(jnp.where(matches, pass_at_k[None, :], 0.0), axis=1, keepdims=True)
    rounded = lax.optimization_barrier(picked.astype(jnp.bfloat16))
    return rounded.astype(jnp.float32)


def COST_DW(m, f, tokens):
    return pl.CostEstimate(flops=CDW * m * f * tokens, bytes_accessed=CDW * (tokens * (m + f) + 2 * m * f), transcendentals=0)


def COST_DX(n, f, width):
    return pl.CostEstimate(flops=CDX * n * f * width, bytes_accessed=CDX * f * (width + n), transcendentals=0)


def after(value, *others):
    return lax.optimization_barrier((value,) + others)[0]


def weight_grad_kernel(place_ref, *refs, n_x, n_s, n_h, rows):
    x_refs, s_refs, out_ref, x_all, s_all = refs[:n_x], refs[n_x:n_x + n_s], refs[-3], refs[-2], refs[-1]
    groups = x_refs[0].shape[0] // rows

    @pl.when(pl.program_id(0) == 0)
    def _():
        for k in range(n_x):
            @pl.when(place_ref[k * groups] >= 0)
            def _(k=k):
                for g in range(groups):
                    start = pl.multiple_of((g * n_h + place_ref[k * groups + g]) * rows, rows)
                    x_all[pl.ds(start, rows), :] = x_refs[k][g * rows:(g + 1) * rows, :]

    start = 0
    for s_ref in s_refs:
        s_all[start:start + s_ref.shape[0], :] = s_ref[...]
        start += s_ref.shape[0]
    out_ref[...] = lax.dot_general(
        x_all[...], s_all[...], (((0,), (0,)), ((), ())), preferred_element_type=jnp.float32
    )


def column_block(f):
    return next((b for b in (1024, 512, 256, 128) if f % b == 0 and f // b > 2), f)


def weight_grad(places, x_pieces, s_pieces, n_h, rows, due):
    x_rows, m = x_pieces[0].shape
    f = s_pieces[0].shape[1]
    tokens = x_rows * n_h
    block = column_block(f)
    body = functools.partial(weight_grad_kernel, n_x=len(x_pieces), n_s=len(s_pieces), n_h=n_h, rows=rows)
    return pl.pallas_call(
        body,
        grid_spec=pltpu.PrefetchScalarGridSpec(
            num_scalar_prefetch=1,
            grid=(f // block,),
            in_specs=[pl.BlockSpec((x_rows, m), lambda j, p: (0, 0))] * len(x_pieces)
            + [pl.BlockSpec((piece.shape[0], block), lambda j, p: (0, j)) for piece in s_pieces],
            out_specs=pl.BlockSpec((m, block), lambda j, p: (0, j)),
            scratch_shapes=[pltpu.VMEM((tokens, m), jnp.bfloat16), pltpu.VMEM((tokens, block), jnp.bfloat16)],
        ),
        out_shape=jax.ShapeDtypeStruct((m, f), jnp.float32),
        compiler_params=pltpu.CompilerParams(vmem_limit_bytes=VMEM),
        cost_estimate=COST_DW(m, f, tokens),
    )(after(places, *due) if due else places, *x_pieces, *s_pieces)


def input_grad_kernel(first_ref, *refs):
    piece_refs, weight_ref, out_ref, tokens = refs[:-3], refs[-3], refs[-2], refs[-1]
    rows = piece_refs[0].shape[0]

    @pl.when(pl.program_id(0) == 0)
    def _():
        for k, piece_ref in enumerate(piece_refs):
            tokens[k * rows:(k + 1) * rows, :] = piece_ref[...]

    share = lax.dot_general(
        tokens[...], weight_ref[...], (((1,), (1,)), ((), ())), preferred_element_type=jnp.float32
    ).astype(out_ref.dtype)
    per_owner = out_ref.shape[2]
    for k in range(out_ref.shape[0]):
        out_ref[k, 0] = share[k * per_owner:(k + 1) * per_owner]


def input_grad(core, n_c, rows, pieces, weight, owners, parts, due):
    d, f = weight.shape
    width = d // n_c
    n = rows * len(pieces)
    part = width // parts
    block = next(b for b in (768, 512, 256, 128, part) if part % b == 0)
    per_part = part // block
    steps = width // block
    first = jnp.stack([core * steps] + [index for _, index in pieces]).astype(jnp.int32)
    return pl.pallas_call(
        input_grad_kernel,
        grid_spec=pltpu.PrefetchScalarGridSpec(
            num_scalar_prefetch=1,
            grid=(steps,),
            in_specs=[pl.BlockSpec((rows, f), lambda j, c, k=k: (c[k + 1], 0)) for k in range(len(pieces))]
            + [pl.BlockSpec((block, f), lambda j, c: (c[0] + j, 0))],
            out_specs=pl.BlockSpec(
                (owners, 1, n // owners, block), lambda j, c: (0, j // per_part, 0, j % per_part)
            ),
            scratch_shapes=[pltpu.VMEM((n, f), jnp.bfloat16)],
        ),
        out_shape=jax.ShapeDtypeStruct((owners, parts, n // owners, part), jnp.bfloat16),
        compiler_params=pltpu.CompilerParams(vmem_limit_bytes=VMEM),
        cost_estimate=COST_DX(n, f, width),
    )(after(first, *due) if due else first, *[piece for piece, _ in pieces], weight)


def make_body(n_h, n_w, n_r):
    n_c = 2 if n_r % 2 == 0 else 1
    n_y = n_r // n_c
    per_w = n_h // n_w

    def slot(w_index, group):
        return group if w_index < n_w // 2 else per_w - 1 - group

    def slot_of(w_index, group):
        return jnp.where(w_index < n_w // 2, group, per_w - 1 - group)

    def replica_perm(dy, dc):
        return [
            (y * n_c + c, (y + dy) % n_y * n_c + (c + dc) % n_c) for y in range(n_y) for c in range(n_c)
        ]

    def over_replica(value, dy, dc):
        return lax.ppermute(value, "replica", replica_perm(dy, dc))

    def over_width(value, dx):
        return lax.ppermute(value, "width", [(w, (w + dx) % n_w) for w in range(n_w)])

    def body(saved_input, grad_out, weight, samples, correct, prompt_ids):
        h, w, r = lax.axis_index("hidden"), lax.axis_index("width"), lax.axis_index("replica")
        y, c = r // n_c, r % n_c
        x_rows, d_half = saved_input.shape
        s_rows, f = grad_out.shape
        rows = s_rows // per_w
        d_core = d_half // n_c
        d_own = d_half // n_r

        parts = []
        for dy in range(n_y):
            for dc in range(n_c):
                target = (y + dy) % n_y * n_c + (c + dc) % n_c
                part = lax.dynamic_slice_in_dim(saved_input, target * d_own, d_own, 1)
                parts.append(part if dy == dc == 0 else over_replica(part, dy, dc))
        x_own = jnp.concatenate(parts, axis=0)

        all_weights = token_weights(prompt_ids, samples, correct)
        scale = lax.dynamic_slice_in_dim(all_weights, w * s_rows, s_rows, 0)
        scaled = (grad_out.astype(jnp.float32) * scale).astype(jnp.bfloat16)

        own_group = [lax.dynamic_slice_in_dim(scaled, slot_of(w, q) * rows, rows, 0) for q in range(per_w)]

        def spread(value, *late):
            value = after(value, *late) if late else value
            return [value] + [over_replica(value, 0, dc) for dc in range(1, n_c)]

        whole = spread(scaled)
        piece, cores = {}, {}

        def send_x(q, *late):
            own = after(own_group[q], *late) if late else own_group[q]
            for dx in range(1, n_w):
                piece[0, dx, q] = over_width(own, dx)

        def send_y(q, *late):
            own = after(own_group[q], *late)
            for dy in range(1, n_y):
                piece[dy, 0, q] = over_replica(own, dy, 0)

        def send_on(q, *late):
            for dy in range(1, n_y):
                for dx in range(1, n_w):
                    if q % 2 == 0:
                        piece[dy, dx, q] = over_width(after(piece[dy, 0, q], *late), dx)
                    else:
                        piece[dy, dx, q] = over_replica(after(piece[0, dx, q], *late), dy, 0)

        def over_x(q):
            return tuple(piece[0, dx, q] for dx in range(1, n_w))

        def over_y(q):
            return tuple(piece[dy, 0, q] for dy in range(1, n_y))

        shares = []

        def share_of(target, choices, come=()):
            target = jnp.clip(target, 0, n_h - 1)
            owner, group = target // per_w, target % per_w
            dx, q = (w - owner) % n_w, slot_of(owner, group)
            picked = None
            for choice in choices:
                share = after(shares[choice], *come) if come else shares[choice]
                value = lax.dynamic_index_in_dim(share, dx, 0, keepdims=False)
                picked = value if picked is None else jnp.where(q == choice, value, picked)
            return picked.reshape(x_own.shape)

        def passes(targets):
            return sorted({slot(t // per_w, t % per_w) for t in targets})

        even = h % 2 == 0
        pairs = [
            [edge for j in range(first, n_h - 1, 2) for edge in ((j, j + 1), (j + 1, j))] for first in range(2)
        ]
        planes = [(h, h >= 0, x_own)]
        came = [x_own, x_own]

        def step_planes(m, *late):
            step, apart = m - 1, n_h - m + 1
            choices = passes([j + apart for j in range(step)] + [j - apart for j in range(apart, n_h)]) if step else []
            come, sent = tuple(came), []
            for kind in range(2):
                to_right = even if kind == 0 else ~even
                value = come[1 - kind] if m < n_h else None
                if step:
                    total = share_of(jnp.where(to_right, h + apart, h - apart), choices, come)
                    if step > 1:
                        total = total + come[1 - kind]
                    is_input = jnp.where(to_right, h >= step, h < apart)
                    value = total if value is None else jnp.where(is_input, value, total)
                sent.append(after(value, *late) if late else value)
            for kind in range(2):
                came[kind] = lax.ppermute(sent[kind], "hidden", pairs[kind])
                from_right = even if kind == 0 else ~even
                if m < n_h:
                    plane = jnp.where(from_right, h + m, h - m)
                    planes.append((plane, (plane >= 0) & (plane < n_h), came[kind]))

        send_x(0)
        step_planes(1)
        came_in = [None, tuple(came)]
        send_y(0, *parts, *whole[1:])
        cut = rows // 2 if rows % 32 == 0 else rows
        for dx in range(1, n_w):
            cores[0, dx, 0] = [piece[0, dx, 0]] + [
                [over_replica(piece[0, dx, 0][i:i + cut], 0, dc) for i in range(0, rows, cut)] for dc in range(1, n_c)
            ]
        for q in range(per_w):
            late = tuple(shares[-1:])
            tokens = []
            for dx in range(n_w):
                for dc in range(n_c):
                    held = cores[0, dx, q][dc] if dx else None
                    for i in range(rows // cut):
                        if not dx:
                            tokens.append((whole[dc], slot_of(w, q) * (rows // cut) + i))
                        elif isinstance(held, list):
                            tokens.append((held[i], w * 0))
                        else:
                            tokens.append((held, w * 0 + i))
            due = late + tuple(parts)
            if q:
                due = late + tuple(came_in[q]) + tuple(cores[dy, 0, q - 1][-1] for dy in range(1, n_y))
            if q + 1 < per_w:
                send_x(q + 1, *whole[1:])
            share = input_grad(c, n_c, cut, tokens, weight, n_w, n_y, due)
            shares.append(share)
            for dy in range(1, n_y):
                cores[dy, 0, q] = spread(piece[dy, 0, q], share)
            if q + 1 < per_w:
                for dx in range(1, n_w):
                    cores[0, dx, q + 1] = spread(piece[0, dx, q + 1], share)
                step_planes(q + 2, *(cores[0, dx, q + 1][-1] for dx in range(1, n_w)))
                came_in.append(tuple(came))
                send_y(q + 1, share, *over_y(q))
                send_on(q, *over_x(q + 1))
        for q in range(per_w - 1, per_w):
            send_on(q, *over_y(q), *over_x(q), *shares[-1:])
        for dy in range(1, n_y):
            for dx in range(1, n_w):
                for q in range(per_w):
                    cores[dy, dx, q] = spread(piece[dy, dx, q])
        for m in range(per_w + 1, n_h):
            step_planes(m)
        due = tuple(came)
        step_planes(n_h)

        places, pieces = [], []
        for plane, there, values in planes:
            owner, group = plane // per_w, plane % per_w
            dx = (w - owner) % n_w
            for dy in range(n_y):
                sent_order = slot_of(owner, group) if dy else jnp.where(dx == 0, group, slot_of(owner, group))
                place = jnp.where(there, dx * per_w + sent_order, -1).astype(jnp.int32)
                places += [place] * n_c
            pieces.append(values)
        s_pieces = []
        for dy in range(n_y):
            for dc in range(n_c):
                for dx in range(n_w):
                    if dy == dx == 0:
                        s_pieces.append(whole[dc])
                    else:
                        for q in range(per_w):
                            held = cores[dy, dx, q][dc]
                            s_pieces += held if isinstance(held, list) else [held]
        places = jnp.stack(places)
        grad_weight = weight_grad(places, pieces, s_pieces, n_h, rows, due)
        came[0] = after(came[0], grad_weight)
        total = share_of(h, range(per_w)).astype(jnp.float32)
        total = total + came[0].astype(jnp.float32) + came[1].astype(jnp.float32)
        total = total.astype(jnp.bfloat16).reshape(n_y, n_c, rows, d_own)
        held = [total[:, 0]] + [over_replica(total[:, dc], 0, n_c - dc) for dc in range(1, n_c)]
        held = jnp.stack(held)
        by_core = [lax.dynamic_index_in_dim(held, (p - c) % n_c, 0, keepdims=False) for p in range(n_c)]
        grad_input = jnp.concatenate([value[k] for value in by_core for k in range(n_y)], axis=1)
        return grad_input, grad_weight

    return body


def solution(mesh):
    in_specs = (
        P(("replica", "hidden"), "width"),
        P(("replica", "width"), "hidden"),
        P("width", "hidden"),
        P(),
        P(),
        P("replica"),
    )
    out_specs = (P(("replica", "hidden"), "width"), P(("width", "replica"), "hidden"))
    body = make_body(mesh.shape["hidden"], mesh.shape["width"], mesh.shape["replica"])
    return jax.shard_map(body, mesh=mesh, in_specs=in_specs, out_specs=out_specs, check_vma=False)
```

```python
import functools

import jax
import jax.numpy as jnp
from jax import lax
from jax.experimental import pallas as pl
from jax.experimental.pallas import tpu as pltpu
from jax.sharding import PartitionSpec as P

K = 4
CDW = 2
CDX = 0
VMEM = 63 << 20


def pass_weights(samples, correct):
    total = samples.astype(jnp.float32)
    good = correct.astype(jnp.float32)
    missing = jnp.ones_like(total)
    for factor_index in range(K):
        missing = missing * jnp.maximum(total - good - factor_index, 0.0) / (total - factor_index)
    return 1.0 - missing


def token_weights(prompt_ids, samples, correct):
    pass_at_k = pass_weights(samples, correct)
    prompt_range = jnp.arange(samples.shape[0], dtype=jnp.int32)
    matches = prompt_ids[:, None] == prompt_range[None, :]
    picked = jnp.sum(jnp.where(matches, pass_at_k[None, :], 0.0), axis=1, keepdims=True)
    rounded = lax.optimization_barrier(picked.astype(jnp.bfloat16))
    return rounded.astype(jnp.float32)


def COST_DW(m, f, tokens):
    return pl.CostEstimate(flops=CDW * m * f * tokens, bytes_accessed=CDW * (tokens * (m + f) + 2 * m * f), transcendentals=0)


def COST_DX(n, f, width):
    return pl.CostEstimate(flops=CDX * n * f * width, bytes_accessed=CDX * f * (width + n), transcendentals=0)


def after(value, *others):
    return lax.optimization_barrier((value,) + others)[0]


def weight_grad_kernel(place_ref, *refs, n_x, n_s, n_h, rows):
    x_refs, s_refs, out_ref, x_all, s_all = refs[:n_x], refs[n_x:n_x + n_s], refs[-3], refs[-2], refs[-1]
    groups = x_refs[0].shape[0] // rows

    @pl.when(pl.program_id(0) == 0)
    def _():
        for k in range(n_x):
            @pl.when(place_ref[k * groups] >= 0)
            def _(k=k):
                for g in range(groups):
                    start = pl.multiple_of((g * n_h + place_ref[k * groups + g]) * rows, rows)
                    x_all[pl.ds(start, rows), :] = x_refs[k][g * rows:(g + 1) * rows, :]

    start = 0
    for s_ref in s_refs:
        s_all[start:start + s_ref.shape[0], :] = s_ref[...]
        start += s_ref.shape[0]
    out_ref[...] = lax.dot_general(
        x_all[...], s_all[...], (((0,), (0,)), ((), ())), preferred_element_type=jnp.float32
    )


def column_block(f):
    return next((b for b in (1024, 512, 256, 128) if f % b == 0 and f // b > 2), f)


def weight_grad(places, x_pieces, s_pieces, n_h, rows, due):
    x_rows, m = x_pieces[0].shape
    f = s_pieces[0].shape[1]
    tokens = x_rows * n_h
    block = column_block(f)
    body = functools.partial(weight_grad_kernel, n_x=len(x_pieces), n_s=len(s_pieces), n_h=n_h, rows=rows)
    return pl.pallas_call(
        body,
        grid_spec=pltpu.PrefetchScalarGridSpec(
            num_scalar_prefetch=1,
            grid=(f // block,),
            in_specs=[pl.BlockSpec((x_rows, m), lambda j, p: (0, 0))] * len(x_pieces)
            + [pl.BlockSpec((piece.shape[0], block), lambda j, p: (0, j)) for piece in s_pieces],
            out_specs=pl.BlockSpec((m, block), lambda j, p: (0, j)),
            scratch_shapes=[pltpu.VMEM((tokens, m), jnp.bfloat16), pltpu.VMEM((tokens, block), jnp.bfloat16)],
        ),
        out_shape=jax.ShapeDtypeStruct((m, f), jnp.float32),
        compiler_params=pltpu.CompilerParams(vmem_limit_bytes=VMEM),
        cost_estimate=COST_DW(m, f, tokens),
    )(after(places, *due) if due else places, *x_pieces, *s_pieces)


def input_grad_kernel(first_ref, *refs):
    piece_refs, weight_ref, out_ref, tokens = refs[:-3], refs[-3], refs[-2], refs[-1]
    rows = piece_refs[0].shape[0]

    @pl.when(pl.program_id(0) == 0)
    def _():
        for k, piece_ref in enumerate(piece_refs):
            tokens[k * rows:(k + 1) * rows, :] = piece_ref[...]

    share = lax.dot_general(
        tokens[...], weight_ref[...], (((1,), (1,)), ((), ())), preferred_element_type=jnp.float32
    ).astype(out_ref.dtype)
    per_owner = out_ref.shape[2]
    for k in range(out_ref.shape[0]):
        out_ref[k, 0] = share[k * per_owner:(k + 1) * per_owner]


def input_grad(core, n_c, rows, pieces, weight, owners, parts, due):
    d, f = weight.shape
    width = d // n_c
    n = rows * len(pieces)
    part = width // parts
    block = next(b for b in (768, 512, 256, 128, part) if part % b == 0)
    per_part = part // block
    steps = width // block
    first = jnp.stack([core * steps] + [index for _, index in pieces]).astype(jnp.int32)
    return pl.pallas_call(
        input_grad_kernel,
        grid_spec=pltpu.PrefetchScalarGridSpec(
            num_scalar_prefetch=1,
            grid=(steps,),
            in_specs=[pl.BlockSpec((rows, f), lambda j, c, k=k: (c[k + 1], 0)) for k in range(len(pieces))]
            + [pl.BlockSpec((block, f), lambda j, c: (c[0] + j, 0))],
            out_specs=pl.BlockSpec(
                (owners, 1, n // owners, block), lambda j, c: (0, j // per_part, 0, j % per_part)
            ),
            scratch_shapes=[pltpu.VMEM((n, f), jnp.bfloat16)],
        ),
        out_shape=jax.ShapeDtypeStruct((owners, parts, n // owners, part), jnp.bfloat16),
        compiler_params=pltpu.CompilerParams(vmem_limit_bytes=VMEM),
        cost_estimate=COST_DX(n, f, width),
    )(after(first, *due) if due else first, *[piece for piece, _ in pieces], weight)


def make_body(n_h, n_w, n_r):
    n_c = 2 if n_r % 2 == 0 else 1
    n_y = n_r // n_c
    per_w = n_h // n_w

    def slot(w_index, group):
        return group if w_index < n_w // 2 else per_w - 1 - group

    def slot_of(w_index, group):
        return jnp.where(w_index < n_w // 2, group, per_w - 1 - group)

    def replica_perm(dy, dc):
        return [
            (y * n_c + c, (y + dy) % n_y * n_c + (c + dc) % n_c) for y in range(n_y) for c in range(n_c)
        ]

    def over_replica(value, dy, dc):
        return lax.ppermute(value, "replica", replica_perm(dy, dc))

    def over_width(value, dx):
        return lax.ppermute(value, "width", [(w, (w + dx) % n_w) for w in range(n_w)])

    def body(saved_input, grad_out, weight, samples, correct, prompt_ids):
        h, w, r = lax.axis_index("hidden"), lax.axis_index("width"), lax.axis_index("replica")
        y, c = r // n_c, r % n_c
        x_rows, d_half = saved_input.shape
        s_rows, f = grad_out.shape
        rows = s_rows // per_w
        d_core = d_half // n_c
        d_own = d_half // n_r

        parts = []
        for dy in range(n_y):
            for dc in range(n_c):
                target = (y + dy) % n_y * n_c + (c + dc) % n_c
                part = lax.dynamic_slice_in_dim(saved_input, target * d_own, d_own, 1)
                parts.append(part if dy == dc == 0 else over_replica(part, dy, dc))
        x_own = jnp.concatenate(parts, axis=0)

        all_weights = token_weights(prompt_ids, samples, correct)
        scale = lax.dynamic_slice_in_dim(all_weights, w * s_rows, s_rows, 0)
        scaled = (grad_out.astype(jnp.float32) * scale).astype(jnp.bfloat16)

        own_group = [lax.dynamic_slice_in_dim(scaled, slot_of(w, q) * rows, rows, 0) for q in range(per_w)]

        def spread(value, *late):
            value = after(value, *late) if late else value
            return [value] + [over_replica(value, 0, dc) for dc in range(1, n_c)]

        whole = spread(scaled)
        piece, cores = {}, {}

        def send_x(q, *late):
            own = after(own_group[q], *late) if late else own_group[q]
            for dx in range(1, n_w):
                piece[0, dx, q] = over_width(own, dx)

        def send_y(q, *late):
            own = after(own_group[q], *late)
            for dy in range(1, n_y):
                piece[dy, 0, q] = over_replica(own, dy, 0)

        def send_on(q, *late):
            for dy in range(1, n_y):
                for dx in range(1, n_w):
                    if q % 2 == 0:
                        piece[dy, dx, q] = over_width(after(piece[dy, 0, q], *late), dx)
                    else:
                        piece[dy, dx, q] = over_replica(after(piece[0, dx, q], *late), dy, 0)

        def over_x(q):
            return tuple(piece[0, dx, q] for dx in range(1, n_w))

        def over_y(q):
            return tuple(piece[dy, 0, q] for dy in range(1, n_y))

        shares = []

        def share_of(target, choices, come=()):
            target = jnp.clip(target, 0, n_h - 1)
            owner, group = target // per_w, target % per_w
            dx, q = (w - owner) % n_w, slot_of(owner, group)
            picked = None
            for choice in choices:
                share = after(shares[choice], *come) if come else shares[choice]
                value = lax.dynamic_index_in_dim(share, dx, 0, keepdims=False)
                picked = value if picked is None else jnp.where(q == choice, value, picked)
            return picked.reshape(x_own.shape)

        def passes(targets):
            return sorted({slot(t // per_w, t % per_w) for t in targets})

        even = h % 2 == 0
        pairs = [
            [edge for j in range(first, n_h - 1, 2) for edge in ((j, j + 1), (j + 1, j))] for first in range(2)
        ]
        planes = [(h, h >= 0, x_own)]
        came = [x_own, x_own]

        def step_planes(m, *late):
            step, apart = m - 1, n_h - m + 1
            choices = passes([j + apart for j in range(step)] + [j - apart for j in range(apart, n_h)]) if step else []
            come, sent = tuple(came), []
            for kind in range(2):
                to_right = even if kind == 0 else ~even
                value = come[1 - kind] if m < n_h else None
                if step:
                    total = share_of(jnp.where(to_right, h + apart, h - apart), choices, come)
                    if step > 1:
                        total = total + come[1 - kind]
                    is_input = jnp.where(to_right, h >= step, h < apart)
                    value = total if value is None else jnp.where(is_input, value, total)
                sent.append(after(value, *late) if late else value)
            for kind in range(2):
                came[kind] = lax.ppermute(sent[kind], "hidden", pairs[kind])
                from_right = even if kind == 0 else ~even
                if m < n_h:
                    plane = jnp.where(from_right, h + m, h - m)
                    planes.append((plane, (plane >= 0) & (plane < n_h), came[kind]))

        send_x(0)
        step_planes(1)
        came_in = [None, tuple(came)]
        send_y(0, *parts, *whole[1:])
        cut = rows // 2 if rows % 32 == 0 else rows
        for dx in range(1, n_w):
            cores[0, dx, 0] = [piece[0, dx, 0]] + [
                [over_replica(piece[0, dx, 0][i:i + cut], 0, dc) for i in range(0, rows, cut)] for dc in range(1, n_c)
            ]
        for q in range(per_w):
            late = tuple(shares[-1:])
            tokens = []
            for dx in range(n_w):
                for dc in range(n_c):
                    held = cores[0, dx, q][dc] if dx else None
                    for i in range(rows // cut):
                        if not dx:
                            tokens.append((whole[dc], slot_of(w, q) * (rows // cut) + i))
                        elif isinstance(held, list):
                            tokens.append((held[i], w * 0))
                        else:
                            tokens.append((held, w * 0 + i))
            due = late + tuple(parts)
            if q:
                due = late + tuple(came_in[q]) + tuple(cores[dy, 0, q - 1][-1] for dy in range(1, n_y))
            if q + 1 < per_w:
                send_x(q + 1, *whole[1:])
            share = input_grad(c, n_c, cut, tokens, weight, n_w, n_y, due)
            shares.append(share)
            for dy in range(1, n_y):
                cores[dy, 0, q] = spread(piece[dy, 0, q], share)
            if q + 1 < per_w:
                for dx in range(1, n_w):
                    cores[0, dx, q + 1] = spread(piece[0, dx, q + 1], share)
                step_planes(q + 2, *(cores[0, dx, q + 1][-1] for dx in range(1, n_w)))
                came_in.append(tuple(came))
                send_y(q + 1, share, *over_y(q))
                send_on(q, *over_x(q + 1))
        for q in range(per_w - 1, per_w):
            send_on(q, *over_y(q), *over_x(q), *shares[-1:])
        for dy in range(1, n_y):
            for dx in range(1, n_w):
                for q in range(per_w):
                    cores[dy, dx, q] = spread(piece[dy, dx, q])
        for m in range(per_w + 1, n_h):
            step_planes(m)
        due = tuple(came)
        step_planes(n_h)

        places, pieces = [], []
        for plane, there, values in planes:
            owner, group = plane // per_w, plane % per_w
            dx = (w - owner) % n_w
            for dy in range(n_y):
                sent_order = slot_of(owner, group) if dy else jnp.where(dx == 0, group, slot_of(owner, group))
                place = jnp.where(there, dx * per_w + sent_order, -1).astype(jnp.int32)
                places += [place] * n_c
            pieces.append(values)
        s_pieces = []
        for dy in range(n_y):
            for dc in range(n_c):
                for dx in range(n_w):
                    if dy == dx == 0:
                        s_pieces.append(whole[dc])
                    else:
                        for q in range(per_w):
                            held = cores[dy, dx, q][dc]
                            s_pieces += held if isinstance(held, list) else [held]
        places = jnp.stack(places)
        grad_weight = weight_grad(places, pieces, s_pieces, n_h, rows, due)
        came[0] = after(came[0], grad_weight)
        total = share_of(h, range(per_w)).astype(jnp.float32)
        total = total + came[0].astype(jnp.float32) + came[1].astype(jnp.float32)
        total = total.astype(jnp.bfloat16).reshape(n_y, n_c, rows, d_own)
        held = [total[:, 0]] + [over_replica(total[:, dc], 0, n_c - dc) for dc in range(1, n_c)]
        held = jnp.stack(held)
        by_core = [lax.dynamic_index_in_dim(held, (p - c) % n_c, 0, keepdims=False) for p in range(n_c)]
        grad_input = jnp.concatenate([value[k] for value in by_core for k in range(n_y)], axis=1)
        return grad_input, grad_weight

    return body


def solution(mesh):
    in_specs = (
        P(("replica", "hidden"), "width"),
        P(("replica", "width"), "hidden"),
        P("width", "hidden"),
        P(),
        P(),
        P("replica"),
    )
    out_specs = (P(("replica", "hidden"), "width"), P(("width", "replica"), "hidden"))
    body = make_body(mesh.shape["hidden"], mesh.shape["width"], mesh.shape["replica"])
    return jax.shard_map(body, mesh=mesh, in_specs=in_specs, out_specs=out_specs, check_vma=False)
```
